128 devices in a mesh: dp: 16 (over x_lo, y, core), opt: 8 (over z, x_hi).
Axes of the slice: x: 4 (x_hi: 2, x_lo: 2; x = x_hi * 2 + x_lo), y: 4, z: 4, core: 2. Of those that a mesh axis runs over, the one named last changes fastest.
Arguments:
- inputs: float32 [32768, 640], P(('dp', 'opt')), may hold values from -6 to 6
- cotangent: float32 [32768, 640], P(('dp', 'opt')), may hold values from -6 to 6
- positions: int32 [32768], P(('dp', 'opt')), may hold values from 0 to 1791, as said below
- w_qkv: float32 [640, 1536], P('opt'), may hold values from -0.25 to 0.25
- w_out: float32 [1024, 640], P('opt'), may hold values from -0.1875 to 0.1875
- w_gate_up: float32 [640, 4096], P('opt'), may hold values from -0.25 to 0.25
- w_down: float32 [2048, 640], P('opt'), may hold values from -0.125 to 0.125
- gains: float32 [3072], P('opt'), may hold values from 0.5 to 1.5
- first_qkv: float32 [640, 1536], P('opt'), may hold values from -128 to 128
- first_out: float32 [1024, 640], P('opt'), may hold values from -128 to 128
- first_gate_up: float32 [640, 4096], P('opt'), may hold values from -128 to 128
- first_down: float32 [2048, 640], P('opt'), may hold values from -128 to 128
- first_gains: float32 [3072], P('opt'), may hold values from -128 to 128
- second_qkv: float32 [640, 1536], P('opt'), may hold values from 32.768 to 131.072
- second_out: float32 [1024, 640], P('opt'), may hold values from 32.768 to 131.072
- second_gate_up: float32 [640, 4096], P('opt'), may hold values from 32.768 to 131.072
- second_down: float32 [2048, 640], P('opt'), may hold values from 32.768 to 131.072
- second_gains: float32 [3072], P('opt'), may hold values from 32.768 to 131.072
Outputs:
- output: float32 [32768, 640], P(('dp', 'opt'))
- input_grad: float32 [32768, 640], P(('dp', 'opt'))
- new_qkv: float32 [640, 1536], P('opt')
- new_out: float32 [1024, 640], P('opt')
- new_gate_up: float32 [640, 4096], P('opt')
- new_down: float32 [2048, 640], P('opt')
- new_gains: float32 [3072], P('opt')
- new_first_qkv: float32 [640, 1536], P('opt')
- new_first_out: float32 [1024, 640], P('opt')
- new_first_gate_up: float32 [640, 4096], P('opt')
- new_first_down: float32 [2048, 640], P('opt')
- new_first_gains: float32 [3072], P('opt')
- new_second_qkv: float32 [640, 1536], P('opt')
- new_second_out: float32 [1024, 640], P('opt')
- new_second_gate_up: float32 [640, 4096], P('opt')
- new_second_down: float32 [2048, 640], P('opt')
- new_second_gains: float32 [3072], P('opt')
The draws below stay inside these ranges and needn't reach their ends.
Inputs may be any that keep to these rules, and one draw needn't show every extreme that they name: `positions`: positions count from 0 at each document's first token; each sequence of 2048 tokens holds three documents: the first and the last together are 256 tokens long, each at least one, and the middle one is 1792 tokens long.
All inputs are finite; a program needn't handle non-finite values.
Results may differ from the reference program's by a relative error of at most 0.034.
Values may be sent and summed in bfloat16 or wider, within the bound.
A program may use at most 128 MiB of HBM per device.

```python
import math
import jax
import jax.numpy as jnp
from jax import lax

D = 640
HQ = 4
HD = 256
FF = 2048
TOK_DEV = 256
STEP = 10
LENGTH = 2048
TOKENS = 32768
QKV = 1536
GAINS = 3072


def draw_positions(key, part):
    key = jax.random.fold_in(key, 7)
    count = TOKENS // LENGTH
    head_len = jax.random.randint(key, (count, 1), 1, TOK_DEV)
    tail_len = TOK_DEV - head_len
    index = jnp.arange(LENGTH, dtype=jnp.int32)[None, :]
    middle_end = LENGTH - tail_len
    starts = jnp.where(index < head_len, 0, jnp.where(index < middle_end, head_len, middle_end))
    return (index - starts).reshape(TOKENS).astype(jnp.int32)


def block_levels(rng, shape, pieces, least, high):
    factor_of, own = 1.0, jax.random.fold_in(rng, 6)
    for dim, shards_of in pieces:
        heights = jnp.exp(jax.random.uniform(jax.random.fold_in(own, dim), (shards_of,), jnp.float32, least / len(pieces), high / len(pieces)))
        factor_of = factor_of * jnp.repeat(heights, shape[dim] // shards_of).reshape([-1 if axis == dim else 1 for axis in range(len(shape))])
    return factor_of


def scatter_about(key, dims, scale, bound, split=(), kind=jnp.bfloat16):
    loudness = block_levels(key, dims, split, -0.22, 0.18) if split else 1.0
    entries = jax.random.normal(key, dims, jnp.float32) * scale * loudness
    return jnp.minimum(jnp.maximum(entries, -bound), bound).astype(kind)


def setup_inputs(seed: int = 0) -> dict:
    streams_of = jax.random.split(jax.random.key(seed), 19)
    inputs = scatter_about(streams_of[0], (TOKENS, D), 1.0, 6.0, ((0, 128),), jnp.float32)
    cotangent = scatter_about(streams_of[1], (TOKENS, D), 1.0, 6.0, ((0, 128),), jnp.float32)
    positions = draw_positions(jax.random.fold_in(streams_of[18], 71), 0)
    w_qkv = scatter_about(streams_of[3], (D, QKV), D ** -0.5, 0.25, ((0, 8),), jnp.float32)
    w_out = scatter_about(streams_of[4], (HQ * HD, D), (HQ * HD) ** -0.5, 0.1875, ((0, 8),), jnp.float32)
    w_gate_up = scatter_about(streams_of[5], (D, 2 * FF), D ** -0.5, 0.25, ((0, 8),), jnp.float32)
    w_down = scatter_about(streams_of[6], (FF, D), FF ** -0.5, 0.125, ((0, 8),), jnp.float32)
    gains = jnp.clip(1.0 + 0.1 * jax.random.normal(streams_of[7], (GAINS,), jnp.float32), 0.5, 1.5)
    first_qkv = scatter_about(streams_of[8], (D, QKV), (0.11 * TOKENS ** 0.5), 128.0, ((0, 8),), jnp.float32)
    first_out = scatter_about(streams_of[9], (HQ * HD, D), (0.11 * TOKENS ** 0.5), 128.0, ((0, 8),), jnp.float32)
    first_gate_up = scatter_about(streams_of[10], (D, 2 * FF), (0.11 * TOKENS ** 0.5), 128.0, ((0, 8),), jnp.float32)
    first_down = scatter_about(streams_of[11], (FF, D), (0.11 * TOKENS ** 0.5), 128.0, ((0, 8),), jnp.float32)
    first_gains = scatter_about(streams_of[12], (GAINS,), (0.11 * TOKENS ** 0.5), 128.0, ((0, 8),), jnp.float32)
    second_qkv = jnp.clip(jnp.exp(math.log(131.072) - 1.3862944 * jax.random.uniform(streams_of[13], (D, QKV), jnp.float32) ** block_levels(streams_of[13], (D, QKV), ((0, 8),), -0.2, 0.2)), 32.768, 131.072)
    second_out = jnp.clip(jnp.exp(math.log(131.072) - 1.3862944 * jax.random.uniform(streams_of[14], (HQ * HD, D), jnp.float32) ** block_levels(streams_of[14], (HQ * HD, D), ((0, 8),), -0.2, 0.2)), 32.768, 131.072)
    second_gate_up = jnp.clip(jnp.exp(math.log(131.072) - 1.3862944 * jax.random.uniform(streams_of[15], (D, 2 * FF), jnp.float32) ** block_levels(streams_of[15], (D, 2 * FF), ((0, 8),), -0.2, 0.2)), 32.768, 131.072)
    second_down = jnp.clip(jnp.exp(math.log(131.072) - 1.3862944 * jax.random.uniform(streams_of[16], (FF, D), jnp.float32) ** block_levels(streams_of[16], (FF, D), ((0, 8),), -0.2, 0.2)), 32.768, 131.072)
    second_gains = jnp.clip(jnp.exp(math.log(131.072) - 1.3862944 * jax.random.uniform(streams_of[17], (GAINS,), jnp.float32) ** block_levels(streams_of[17], (GAINS,), ((0, 8),), -0.2, 0.2)), 32.768, 131.072)
    return {"inputs": inputs, "cotangent": cotangent, "positions": positions, "w_qkv": w_qkv, "w_out": w_out, "w_gate_up": w_gate_up, "w_down": w_down, "gains": gains, "first_qkv": first_qkv, "first_out": first_out, "first_gate_up": first_gate_up, "first_down": first_down, "first_gains": first_gains, "second_qkv": second_qkv, "second_out": second_out, "second_gate_up": second_gate_up, "second_down": second_down, "second_gains": second_gains}


norm_epsilon = 1e-06

@jax.custom_vjp
def low(v):
    return lax.optimization_barrier(v.astype(jnp.bfloat16)).astype(jnp.float32)

@jax.custom_vjp
def low_back(v):
    return v

def low_keep(v):
    return (low(v), None)

def low_pass(kept, grad):
    return (grad,)

def back_keep(v):
    return (v, None)

def back_low(kept, grad):
    return (low(grad),)
low.defvjp(low_keep, low_pass)
low_back.defvjp(back_keep, back_low)

def matmul(left, right):
    return jnp.dot(left, right, precision=lax.Precision.HIGHEST, preferred_element_type=jnp.float32)

def rms_norm(values):
    return values * lax.rsqrt(lax.optimization_barrier(jnp.mean(values * values, axis=-1, keepdims=True)) + norm_epsilon)

def scale_norm(values, scale_gain):
    return rms_norm(values) * scale_gain

def add_norm(residual, values, scale_gain):
    return residual + rms_norm(values) * scale_gain

def rotary_tables(positions):
    freqs = 1000000.0 ** (-(jnp.arange(HD // 2, dtype=jnp.float32) * 2.0 / HD))
    angles = positions.astype(jnp.float32)[:, None] * freqs[None, :]
    return (jnp.cos(angles), jnp.sin(angles))

def rotate(values, cosine, sine_part):
    halfway = values.shape[-1] // 2
    first_half = values[..., :halfway]
    second_half = values[..., halfway:]
    return jnp.concatenate([first_half * cosine - second_half * sine_part, second_half * cosine + first_half * sine_part], axis=-1)

def split_heads(projected, query_gain, key_gain, cosine, sine_part):
    width = HQ * HD
    queries = projected[:, :width].reshape(projected.shape[0], HQ, HD)
    keys = projected[:, width:width + HD]
    values = projected[:, width + HD:]
    queries = rotate(rms_norm(queries) * query_gain, cosine[:, None, :], sine_part[:, None, :])
    keys = rotate(rms_norm(keys) * key_gain, cosine, sine_part)
    return (queries, keys, values)

def gated(projected):
    return jax.nn.gelu(projected[:, :FF], approximate=True) * projected[:, FF:]

def split_gains(gain_all):
    return (gain_all[:D], gain_all[D:2 * D], gain_all[2 * D:3 * D], gain_all[3 * D:4 * D], gain_all[4 * D:4 * D + HD], gain_all[4 * D + HD:])

@jax.checkpoint
def attend(queries, keys, values, positions):
    length = keys.shape[0]
    index = jnp.arange(length, dtype=jnp.int32)
    offset = index[:, None] - index[None, :]
    allowed = (offset >= 0) & (offset <= positions[:, None])
    scores = jnp.einsum('thd,ud->htu', queries, keys, precision=lax.Precision.HIGHEST) * HD ** (-0.5)
    scores = low_back(scores)
    scores = jnp.where(allowed[None], scores, -1e+30)
    total = jax.nn.logsumexp(scores, axis=-1, keepdims=True)
    weights = low(jnp.exp(scores - total))
    return jnp.einsum('htu,ud->thd', weights, values, precision=lax.Precision.HIGHEST)

def forward(block_in, positions, w_qkv, w_out, w_gate_up, w_down, gains):
    g_attn, g_post, g_ffn, g_out, g_query, g_key = split_gains(low(gains))
    cosine, sine_part = rotary_tables(positions)
    normed = low(scale_norm(block_in, g_attn))
    projected = low_back(matmul(normed, low(w_qkv)))
    queries, keys, values = split_heads(projected, g_query, g_key, cosine, sine_part)
    mixed = attend(low(queries), low(keys), low(values), positions)
    mixed = low(low_back(mixed.reshape(mixed.shape[0], HQ * HD)))
    branch = low_back(matmul(mixed, low(w_out)))
    middle = add_norm(block_in, branch, g_post)
    ffn_in = low(scale_norm(middle, g_ffn))
    gate_up = low_back(matmul(ffn_in, low(w_gate_up)))
    hidden = low(gated(gate_up))
    down_proj = low_back(matmul(hidden, low(w_down)))
    return add_norm(middle, down_proj, g_out)

def adamw(weight, gradient, first, second, step_rate, weight_decay):
    new_first = 0.9 * first + 0.1 * gradient
    new_second = 0.999 * second + 0.001 * gradient * gradient
    first_hat = new_first / (1.0 - 0.9 ** STEP)
    second_hat = new_second / (1.0 - 0.999 ** STEP)
    new_weight = weight - step_rate * (first_hat / (jnp.sqrt(second_hat) + 1e-08) + weight_decay * weight)
    return (new_weight, new_first, new_second)

def reference(inputs, cotangent, positions, w_qkv, w_out, w_gate_up, w_down, gains, first_qkv, first_out, first_gate_up, first_down, first_gains, second_qkv, second_out, second_gate_up, second_down, second_gains):
    seq_in = inputs.reshape(-1, LENGTH, D)
    seq_grad = cotangent.reshape(-1, LENGTH, D)
    seq_pos = positions.reshape(-1, LENGTH)
    params = (w_qkv, w_out, w_gate_up, w_down, gains)
    zeros = tuple((jnp.zeros_like(param) for param in params))

    def one_sequence(carry, item):
        block_in, block_grad, block_pos = item

        def run(values, p_qkv, p_out, p_gate_up, p_down, p_gains):
            return forward(values, block_pos, p_qkv, p_out, p_gate_up, p_down, p_gains)
        result, pull = jax.vjp(run, block_in, w_qkv, w_out, w_gate_up, w_down, gains)
        grads = pull(block_grad)
        summed = tuple((total + piece for total, piece in zip(carry, grads[1:])))
        return (summed, (result, grads[0]))
    totals, (outs, back) = lax.scan(one_sequence, zeros, (seq_in, seq_grad, seq_pos))
    rates = (D ** (-0.5), (HQ * HD) ** (-0.5), D ** (-0.5), FF ** (-0.5), 0.8)
    decays = (0.01, 0.01, 0.01, 0.01, 0.0)
    firsts = (first_qkv, first_out, first_gate_up, first_down, first_gains)
    seconds = (second_qkv, second_out, second_gate_up, second_down, second_gains)
    updated = [adamw(params[idx], totals[idx], firsts[idx], seconds[idx], rates[idx], decays[idx]) for idx in range(5)]
    return (outs.reshape(-1, D), back.reshape(-1, D), updated[0][0], updated[1][0], updated[2][0], updated[3][0], updated[4][0], updated[0][1], updated[1][1], updated[2][1], updated[3][1], updated[4][1], updated[0][2], updated[1][2], updated[2][2], updated[3][2], updated[4][2])
```

```python
import functools

import jax
import jax.numpy as jnp
from jax import lax
from jax.experimental import pallas as pl
from jax.experimental.pallas import tpu as pltpu
from jax.sharding import PartitionSpec as P

D = 640
HQ = 4
HD = 256
FF = 2048
STEP = 10


norm_epsilon = 1e-06


MESH = pl.DeviceIdType.MESH
TENSORS = {
    "qkv": dict(rows=80, cols=1536, dim=1, kind=jnp.bfloat16),
    "out": dict(rows=128, cols=640, dim=0, kind=jnp.bfloat16),
    "gu": dict(rows=80, cols=4096, dim=1, kind=jnp.bfloat16),
    "down": dict(rows=256, cols=640, dim=0, kind=jnp.bfloat16),
    "gain": dict(rows=32, cols=128, dim=0, kind=jnp.float32),
}


class Place:
    def __init__(self):
        dp, opt = lax.axis_index("dp"), lax.axis_index("opt")
        self.xl, self.y, self.c = dp // 8, (dp // 2) % 4, dp % 2
        self.z, self.xh = opt // 2, opt % 2
        self.x = self.xh * 2 + self.xl

    def device(self, xl=None, y=None, c=None, z=None, xh=None):
        xl = self.xl if xl is None else xl
        y = self.y if y is None else y
        c = self.c if c is None else c
        z = self.z if z is None else z
        xh = self.xh if xh is None else xh
        return ((xl * 4 + y) * 2 + c, z * 2 + xh)

    def on_z(self, k):
        z = (self.z + k) % 4
        return z, self.device(z=z)

    def on_y(self, k):
        y = (self.y + k) % 4
        return y, self.device(y=y)

    def on_x(self, k):
        x = (self.x + k) % 4
        return (x // 2, x % 2), self.device(xh=x // 2, xl=x % 2)

    def other_core(self):
        return self.device(c=1 - self.c)

    def pair(self):
        return self.device(xl=1 - self.xl)


def greet(devices):
    barrier = pltpu.get_barrier_semaphore()
    for device in devices:
        pl.semaphore_signal(barrier, inc=1, device_id=device, device_id_type=MESH)
    pl.semaphore_wait(barrier, len(devices))


def cut(ref, name, lead, start, size):
    dim = TENSORS[name]["dim"]
    if isinstance(start, int):
        window = pl.ds(start, size)
    else:
        window = pl.ds(pl.multiple_of(start, 128 if dim else (16 if name != "gain" else 8)), size)
    if dim:
        return ref.at[(*lead, slice(None), window)]
    return ref.at[(*lead, window)]


class Copies:
    def __init__(self, send, recv):
        self.send, self.recv, self.used = send, recv, 0

    def remote(self, src, dst, device):
        i = self.used
        self.used += 1
        copy = pltpu.make_async_remote_copy(
            src_ref=src,
            dst_ref=dst,
            send_sem=self.send.at[i],
            recv_sem=self.recv.at[i],
            device_id=device,
            device_id_type=MESH,
        )
        copy.start()
        return copy

    def here(self, src, dst):
        i = self.used
        self.used += 1
        copy = pltpu.make_async_copy(src, dst, self.send.at[i])
        copy.start()
        return copy


GATHER = ("qkv", "gain", "out", "gu", "down")
ORDER = {"qkv": "xz", "gain": "xz", "out": "xz", "down": "zx", "gu": "zxy"}
K3 = (1, 2, 3)


def gather_steps(at, copies, name, shard, full):
    spec = TENSORS[name]
    unit = spec["rows" if spec["dim"] == 0 else "cols"] // 4
    every = slice(None)
    z, xh, xl, y, c = at.z, at.xh, at.xl, at.y, at.c
    order = ORDER[name]
    started = []

    def send(view, device):
        started.append(copies.remote(view, view, device))
        return started[-1]

    if order == "zxy":
        sub = unit // 4
        own = c * (8 * sub) + y * (2 * sub) + xl * sub
        size = sub
    else:
        own = (c * 2 + xl) * unit
        size = unit
    mine = cut(shard, name, (), own, size)
    here = copies.here(mine, cut(full, name, (z, xh), own, size))
    land = cut(full, name, (z, xh), own, size)
    first = []
    for k in K3:
        device = at.on_x(k)[1] if order == "xz" else at.on_z(k)[1]
        first.append(copies.remote(mine, land, device))
    started.extend(first)
    yield
    here.wait()
    for copy in first:
        copy.wait_recv()
    if order == "xz":
        view = cut(full, name, (z, every), c * 2 * unit, 2 * unit)
        second = [send(view, at.on_z(k)[1]) for k in K3]
        last = [send(view, at.other_core())]
        yield
        for copy, k in zip(second, K3):
            copy.wait_recv()
            zz = (z - k) % 4
            last.append(send(cut(full, name, (zz, every), c * 2 * unit, 2 * unit), at.other_core()))
    elif order == "zx":
        view = cut(full, name, (every, xh), own, size)
        second = [send(view, at.on_x(k)[1]) for k in K3]
        last = [send(view, at.other_core())]
        yield
        for copy, k in zip(second, K3):
            copy.wait_recv()
            xx = (at.x - k) % 4
            view = cut(full, name, (every, xx // 2), (c * 2 + xx % 2) * unit, size)
            last.append(send(view, at.other_core()))
    else:
        view = cut(full, name, (every, xh), own, size)
        second = [send(view, at.on_x(k)[1]) for k in K3]
        yield
        for copy in second:
            copy.wait_recv()
        wide = 2 * sub
        view = cut(full, name, (every, every), c * (8 * sub) + y * wide, wide)
        third = [send(view, at.on_y(k)[1]) for k in K3]
        last = [send(view, at.other_core())]
        yield
        for copy, k in zip(third, K3):
            copy.wait_recv()
            yy = (y - k) % 4
            view = cut(full, name, (every, every), c * (8 * sub) + yy * wide, wide)
            last.append(send(view, at.other_core()))
    yield
    for copy in last:
        copy.wait_recv()
    for copy in started:
        copy.wait_send()


def run_all(steps):
    steps = list(steps)
    while steps:
        left = []
        for step in steps:
            try:
                next(step)
                left.append(step)
            except StopIteration:
                pass
        steps = left


def everyone(at):
    found = [at.other_core()]
    for k in K3:
        found += [at.on_z(k)[1], at.on_x(k)[1], at.on_y(k)[1]]
    return found


def gather_kernel(names, *refs):
    n = len(names)
    shards, fulls, (send, recv) = refs[:n], refs[n : 2 * n], refs[2 * n :]
    at = Place()
    greet(everyone(at))
    copies = Copies(send, recv)
    run_all(gather_steps(at, copies, name, s, f) for name, s, f in zip(names, shards, fulls))


def gather_weights(shards):
    names = GATHER
    where = pl.BlockSpec(memory_space=pltpu.HBM)
    count = 16 * len(names)
    outs = pl.pallas_call(
        functools.partial(gather_kernel, names),
        name="gather_weights",
        out_shape=[
            jax.ShapeDtypeStruct((4, 2, TENSORS[t]["rows"], TENSORS[t]["cols"]), TENSORS[t]["kind"])
            for t in names
        ],
        in_specs=[where] * len(names),
        out_specs=[where] * len(names),
        scratch_shapes=[pltpu.SemaphoreType.DMA((count,)), pltpu.SemaphoreType.DMA((count,))],
        compiler_params=pltpu.CompilerParams(collective_id=1, has_side_effects=True),
    )(*[shards[t] for t in names])
    return dict(zip(names, outs))


def group_devices(at):
    me = at.z * 2 + at.xh
    found = []
    for k in range(1, 8):
        opt = (me + k) % 8
        found.append((opt, at.device(z=opt // 2, xh=opt % 2)))
    return found


def collect_kernel(mine, full, send, recv):
    at = Place()
    peers = group_devices(at)
    greet([device for _, device in peers])
    copies = Copies(send, recv)
    me = at.z * 2 + at.xh
    here = copies.here(mine, full.at[me])
    going = [copies.remote(mine, full.at[me], device) for _, device in peers]
    here.wait()
    for copy in going:
        copy.wait()


def collect_rows(mine):
    where = pl.BlockSpec(memory_space=pltpu.HBM)
    return pl.pallas_call(
        collect_kernel,
        name="collect_key_values",
        out_shape=jax.ShapeDtypeStruct((8, *mine.shape), mine.dtype),
        in_specs=[where],
        out_specs=where,
        scratch_shapes=[pltpu.SemaphoreType.DMA((8,)), pltpu.SemaphoreType.DMA((8,))],
        compiler_params=pltpu.CompilerParams(collective_id=2, has_side_effects=True),
    )(mine)


def deliver_kernel(parts, total, landed, send, recv):
    at = Place()
    peers = group_devices(at)
    greet([device for _, device in peers])
    copies = Copies(send, recv)
    me = at.z * 2 + at.xh
    going = [
        copies.remote(parts.at[opt], landed.at[i], device) for i, (opt, device) in enumerate(peers)
    ]
    total[...] = parts[me].astype(jnp.float32)
    for i, copy in enumerate(going):
        copy.wait_recv()
        total[...] += landed[i].astype(jnp.float32)
    for copy in going:
        copy.wait_send()


def deliver_rows(parts):
    vmem = pl.BlockSpec(memory_space=pltpu.VMEM)
    return pl.pallas_call(
        deliver_kernel,
        name="deliver_key_values",
        out_shape=jax.ShapeDtypeStruct(parts.shape[1:], jnp.float32),
        in_specs=[vmem],
        out_specs=vmem,
        scratch_shapes=[
            pltpu.VMEM((7, *parts.shape[1:]), parts.dtype),
            pltpu.SemaphoreType.DMA((8,)),
            pltpu.SemaphoreType.DMA((8,)),
        ],
        compiler_params=pltpu.CompilerParams(
            collective_id=3, has_side_effects=True, vmem_limit_bytes=40 * 2**20
        ),
    )(parts)


SUM = ("gu", "down", "out", "qkv", "gain")
SUM_ORDER = {"qkv": "zxy", "gain": "zxy", "out": "zxy", "down": "xzy", "gu": "yxz"}


def shaped(name, lead, split):
    spec = TENSORS[name]
    rows, cols = spec["rows"], spec["cols"]
    if spec["dim"]:
        return (*lead, rows, cols // split)
    return (*lead, rows // split, cols)


def sum_scratch(name):
    kind = TENSORS[name]["kind"]
    order = SUM_ORDER[name]
    if order == "zxy":
        shapes = [((4, 2), 2), ((3, 2), 2), ((2,), 2), ((3,), 4), ((), 4), ((3,), 4)]
    elif order == "xzy":
        shapes = [((4, 2), 2), ((3, 4), 4), ((4,), 4), ((3,), 4), ((), 4), ((3,), 4)]
    else:
        shapes = [((4, 2), 2), ((3, 4, 2), 8), ((4, 2), 8), ((3, 4), 16), ((4,), 16), ((3,), 16)]
    return [pltpu.VMEM(shaped(name, lead, split), kind) for lead, split in shapes]


def sum_steps(at, copies, name, grad, result, landed, land1, sum1, land2, sum2, land3):
    spec = TENSORS[name]
    order = SUM_ORDER[name]
    kind = spec["kind"]
    unit = spec["rows" if spec["dim"] == 0 else "cols"] // 4
    half = 2 * unit
    every = slice(None)
    z, xh, xl, y, c = at.z, at.xh, at.xl, at.y, at.c
    f32 = jnp.float32
    started = []

    def send(src, dst, device):
        started.append(copies.remote(src, dst, device))
        return started[-1]

    def add(own, arrived, target):
        value = own[...].astype(f32)
        for ref in arrived:
            value = value + ref[...].astype(f32)
        target[...] = value.astype(kind)

    swap = send(cut(grad, name, (every, every), (1 - c) * half, half), landed, at.other_core())
    yield
    swap.wait_recv()

    def joined(i, carry):
        a, b = i // 2, i % 2
        add(cut(grad, name, (a, b), c * half, half), [landed.at[a, b]], landed.at[a, b])
        return carry

    lax.fori_loop(0, 8, joined, 0)
    if order == "zxy":
        first = [send(landed.at[at.on_z(k)[0]], land1.at[k - 1], at.on_z(k)[1]) for k in K3]
        yield
        for copy in first:
            copy.wait_recv()
        for b in range(2):
            add(landed.at[z, b], [land1.at[i, b] for i in range(3)], sum1.at[b])
        second = []
        for k in K3:
            (xxh, xxl), device = at.on_x(k)
            second.append(send(cut(sum1, name, (xxh,), xxl * unit, unit), land2.at[k - 1], device))
        yield
        for copy in second:
            copy.wait_recv()
        add(cut(sum1, name, (xh,), xl * unit, unit), [land2.at[i] for i in range(3)], sum2)
    elif order == "xzy":
        first = []
        for k in K3:
            (xxh, xxl), device = at.on_x(k)
            first.append(
                send(cut(landed, name, (every, xxh), xxl * unit, unit), land1.at[k - 1], device)
            )
        yield
        for copy in first:
            copy.wait_recv()
        for a in range(4):
            add(
                cut(landed, name, (a, xh), xl * unit, unit),
                [land1.at[i, a] for i in range(3)],
                sum1.at[a],
            )
        second = [send(sum1.at[at.on_z(k)[0]], land2.at[k - 1], at.on_z(k)[1]) for k in K3]
        yield
        for copy in second:
            copy.wait_recv()
        add(sum1.at[z], [land2.at[i] for i in range(3)], sum2)
    else:
        sub = unit // 4
        first = []
        for k in K3:
            yy, device = at.on_y(k)
            first.append(
                send(cut(landed, name, (every, every), yy * 2 * sub, 2 * sub), land1.at[k - 1], device)
            )
        yield
        for copy in first:
            copy.wait_recv()

        def over(i, carry):
            a, b = i // 2, i % 2
            add(
                cut(landed, name, (a, b), y * 2 * sub, 2 * sub),
                [land1.at[j, a, b] for j in range(3)],
                sum1.at[a, b],
            )
            return carry

        lax.fori_loop(0, 8, over, 0)
        second = []
        for k in K3:
            (xxh, xxl), device = at.on_x(k)
            second.append(send(cut(sum1, name, (every, xxh), xxl * sub, sub), land2.at[k - 1], device))
        yield
        for copy in second:
            copy.wait_recv()
        for a in range(4):
            add(
                cut(sum1, name, (a, xh), xl * sub, sub),
                [land2.at[i, a] for i in range(3)],
                sum2.at[a],
            )
        third = [send(sum2.at[at.on_z(k)[0]], land3.at[k - 1], at.on_z(k)[1]) for k in K3]
        yield
        for copy in third:
            copy.wait_recv()
        place = c * (8 * sub) + y * (2 * sub) + xl * sub
        mine = cut(result, name, (), place, sub)
        add(sum2.at[z], [land3.at[i] for i in range(3)], mine)
        near = send(mine, mine, at.pair())
        yield
        near.wait_recv()
        wide = cut(result, name, (), c * (8 * sub) + y * (2 * sub), 2 * sub)
        around = [send(wide, wide, at.on_y(k)[1]) for k in K3]
        yield
        for copy in around:
            copy.wait_recv()
    if order != "yxz":
        third = [send(sum2, land3.at[k - 1], at.on_y(k)[1]) for k in K3]
        yield
        for copy in third:
            copy.wait_recv()
        mine = cut(result, name, (), (c * 2 + xl) * unit, unit)
        add(sum2, [land3.at[i] for i in range(3)], mine)
        near = send(mine, mine, at.pair())
        yield
        near.wait_recv()
    whole = cut(result, name, (), c * half, half)
    across = send(whole, whole, at.other_core())
    yield
    across.wait_recv()
    for copy in started:
        copy.wait_send()


def sum_kernel(names, *refs):
    n = len(names)
    grads, results, rest = refs[:n], refs[n : 2 * n], refs[2 * n :]
    send, recv = rest[-2:]
    at = Place()
    greet(everyone(at))
    copies = Copies(send, recv)
    run_all(
        sum_steps(at, copies, name, g, r, *rest[6 * i : 6 * i + 6])
        for i, (name, g, r) in enumerate(zip(names, grads, results))
    )


def sum_grads(grads):
    names = SUM
    vmem = pl.BlockSpec(memory_space=pltpu.VMEM)
    scratch = []
    for t in names:
        scratch += sum_scratch(t)
    count = 16 * len(names)
    outs = pl.pallas_call(
        functools.partial(sum_kernel, names),
        name="sum_grads",
        out_shape=[
            jax.ShapeDtypeStruct((TENSORS[t]["rows"], TENSORS[t]["cols"]), TENSORS[t]["kind"])
            for t in names
        ],
        in_specs=[vmem] * len(names),
        out_specs=[vmem] * len(names),
        scratch_shapes=scratch
        + [pltpu.SemaphoreType.DMA((count,)), pltpu.SemaphoreType.DMA((count,))],
        compiler_params=pltpu.CompilerParams(
            collective_id=4, has_side_effects=True, vmem_limit_bytes=56 * 2**20
        ),
    )(*[grads[t] for t in names])
    return dict(zip(names, outs))


def spread_gains(values):
    lead = values.shape[:-1]
    rows = values.reshape(*lead, 3, 1, 128)
    rows = jnp.pad(rows, [(0, 0)] * len(lead) + [(0, 1), (0, 7), (0, 0)])
    return rows.reshape(*lead, 32, 128)


def packed_gains(rows):
    lead = rows.shape[:-2]
    return rows.reshape(*lead, 4, 8, 128)[..., :3, 0, :].reshape(*lead, 384)


def rms_norm(values):
    return values * lax.rsqrt(jnp.mean(values * values, axis=-1, keepdims=True) + norm_epsilon)


def scale_norm(values, scale_gain):
    return rms_norm(values) * scale_gain


def add_norm(residual, values, scale_gain):
    return residual + rms_norm(values) * scale_gain


def rotary_tables(positions):
    freqs = 1000000.0 ** (-(jnp.arange(HD // 2, dtype=jnp.float32) * 2.0 / HD))
    angles = positions.astype(jnp.float32)[:, None] * freqs[None, :]
    return (jnp.cos(angles), jnp.sin(angles))


def rotate(values, cosine, sine_part):
    halfway = values.shape[-1] // 2
    first_half = values[..., :halfway]
    second_half = values[..., halfway:]
    return jnp.concatenate(
        [
            first_half * cosine - second_half * sine_part,
            second_half * cosine + first_half * sine_part,
        ],
        axis=-1,
    )


def split_heads(projected, query_gain, key_gain, cosine, sine_part):
    width = HQ * HD
    queries = projected[:, :width].reshape(projected.shape[0], HQ, HD)
    keys = projected[:, width : width + HD]
    values = projected[:, width + HD :]
    queries = rotate(rms_norm(queries) * query_gain, cosine[:, None, :], sine_part[:, None, :])
    keys = rotate(rms_norm(keys) * key_gain, cosine, sine_part)
    return (queries, keys, values)


def gated(projected):
    return jax.nn.gelu(projected[:, :FF], approximate=True) * projected[:, FF:]


def split_gains(gain_all):
    return (
        gain_all[:D],
        gain_all[D : 2 * D],
        gain_all[2 * D : 3 * D],
        gain_all[3 * D : 4 * D],
        gain_all[4 * D : 4 * D + HD],
        gain_all[4 * D + HD :],
    )


def block_scores(query_block, index_block, position_block, key_values):
    keys = key_values[:, :HD]
    scores = jnp.einsum(
        "thd,ud->htu", query_block, keys, preferred_element_type=jnp.float32
    ) * HD ** (-0.5)
    key_index = jnp.arange(key_values.shape[0], dtype=jnp.int32)
    offset = index_block[:, None] - key_index[None, :]
    allowed = (offset >= 0) & (offset <= position_block[:, None])
    return jnp.where(allowed[None], scores, -1e30)


def attend_forward(query_blocks, index_blocks, position_blocks, key_values):
    values = key_values[:, HD:]

    def one_block(item):
        query_block, index_block, position_block = item
        scores = block_scores(query_block, index_block, position_block, key_values)
        total = jax.nn.logsumexp(scores, axis=-1, keepdims=True)
        weights = jnp.exp(scores - total).astype(jnp.bfloat16)
        mixed = jnp.einsum("htu,ud->thd", weights, values, preferred_element_type=jnp.float32)
        return (mixed.astype(jnp.bfloat16), total)

    return lax.map(one_block, (query_blocks, index_blocks, position_blocks))


def attend_backward(query_blocks, grad_blocks, index_blocks, position_blocks, totals, key_values):
    keys = key_values[:, :HD]
    values = key_values[:, HD:]

    def one_block(carry, item):
        query_block, grad_block, index_block, position_block, total = item
        scores = block_scores(query_block, index_block, position_block, key_values)
        weights = jnp.exp(scores - total)
        weights_low = weights.astype(jnp.bfloat16)
        grad_weights = jnp.einsum(
            "thd,ud->htu", grad_block, values, preferred_element_type=jnp.float32
        )
        inner = jnp.sum(grad_weights * weights, axis=-1, keepdims=True)
        grad_scores = (weights * (grad_weights - inner)).astype(jnp.bfloat16)
        grad_query = jnp.einsum(
            "htu,ud->thd", grad_scores, keys, preferred_element_type=jnp.float32
        ) * HD ** (-0.5)
        grad_keys = jnp.einsum(
            "htu,thd->ud", grad_scores, query_block, preferred_element_type=jnp.float32
        ) * HD ** (-0.5)
        grad_values = jnp.einsum(
            "htu,thd->ud", weights_low, grad_block, preferred_element_type=jnp.float32
        )
        return (carry + jnp.concatenate([grad_keys, grad_values], axis=-1), grad_query)

    start = jnp.zeros((key_values.shape[0], 2 * HD), jnp.float32)
    return lax.scan(
        one_block, start, (query_blocks, grad_blocks, index_blocks, position_blocks, totals)
    )


def adamw(weight, gradient, first, second, step_rate, weight_decay):
    new_first = 0.9 * first + 0.1 * gradient
    new_second = 0.999 * second + 0.001 * gradient * gradient
    first_hat = new_first / (1.0 - 0.9**STEP)
    second_hat = new_second / (1.0 - 0.999**STEP)
    new_weight = weight - step_rate * (
        first_hat / (jnp.sqrt(second_hat) + 1e-08) + weight_decay * weight
    )
    return (new_weight, new_first, new_second)


def local(
    inputs,
    cotangent,
    positions,
    w_qkv,
    w_out,
    w_gate_up,
    w_down,
    gains,
    first_qkv,
    first_out,
    first_gate_up,
    first_down,
    first_gains,
    second_qkv,
    second_out,
    second_gate_up,
    second_down,
    second_gains,
):
    tokens = inputs.shape[0]
    bf_type = jnp.bfloat16
    full = gather_weights(
        {
            "qkv": w_qkv.astype(bf_type),
            "out": w_out.astype(bf_type),
            "gu": w_gate_up.astype(bf_type),
            "down": w_down.astype(bf_type),
            "gain": spread_gains(gains.astype(bf_type).astype(jnp.float32)),
        }
    )
    wq_full = full["qkv"].reshape(D, (HQ + 2) * HD)
    wo_full = full["out"].reshape(HQ * HD, D)
    wgu_full = full["gu"].reshape(D, 2 * FF)
    wd_full = full["down"].reshape(FF, D)
    gain_full = packed_gains(full["gain"]).reshape(-1)
    g_attn, g_post, g_ffn, g_out, g_query, g_key = split_gains(gain_full.astype(jnp.float32))
    cosine, sine_part = rotary_tables(positions)
    normed, pre_pull = jax.vjp(scale_norm, inputs, g_attn)
    normed_low = normed.astype(bf_type)
    projected = jnp.dot(normed_low, wq_full, preferred_element_type=jnp.float32)

    def heads_of(proj_values, query_gain, key_gain):
        return split_heads(proj_values, query_gain, key_gain, cosine, sine_part)

    (queries, keys, values), heads_pull = jax.vjp(heads_of, projected, g_query, g_key)
    queries_low = queries.astype(bf_type)
    key_values = jnp.concatenate([keys, values], axis=-1).astype(bf_type)
    all_key_values = collect_rows(key_values).reshape(-1, 2 * HD)
    block = min(tokens, 128)
    blocks = tokens // block
    query_index = lax.axis_index("opt") * tokens + jnp.arange(tokens, dtype=jnp.int32)
    query_blocks = queries_low.reshape(blocks, block, HQ, HD)
    index_blocks = query_index.reshape(blocks, block)
    position_blocks = positions.reshape(blocks, block)
    mixed_blocks, totals = attend_forward(
        query_blocks, index_blocks, position_blocks, all_key_values
    )
    mixed_low = mixed_blocks.reshape(tokens, HQ * HD)
    branch = jnp.dot(mixed_low, wo_full, preferred_element_type=jnp.float32)
    middle, post_pull = jax.vjp(add_norm, inputs, branch, g_post)
    ffn_in, ffn_pull = jax.vjp(scale_norm, middle, g_ffn)
    ffn_low = ffn_in.astype(bf_type)
    gate_up = jnp.dot(ffn_low, wgu_full, preferred_element_type=jnp.float32)
    hidden, act_pull = jax.vjp(gated, gate_up)
    hidden_low = hidden.astype(bf_type)
    down_proj = jnp.dot(hidden_low, wd_full, preferred_element_type=jnp.float32)
    output, out_pull = jax.vjp(add_norm, middle, down_proj, g_out)
    middle_grad, down_grad, grad_g_out = out_pull(cotangent)
    down_low = down_grad.astype(bf_type)
    grad_down = jnp.einsum("tf,td->fd", hidden_low, down_low, preferred_element_type=jnp.float32)
    hidden_grad = jnp.einsum("td,fd->tf", down_low, wd_full, preferred_element_type=jnp.float32)
    (gate_up_grad,) = act_pull(hidden_grad)
    gate_up_low = gate_up_grad.astype(bf_type)
    grad_gate_up = jnp.einsum("td,tf->df", ffn_low, gate_up_low, preferred_element_type=jnp.float32)
    ffn_grad = jnp.einsum("tf,df->td", gate_up_low, wgu_full, preferred_element_type=jnp.float32)
    middle_more, grad_g_ffn = ffn_pull(ffn_grad)
    middle_grad = middle_grad + middle_more
    input_first, branch_grad, grad_g_post = post_pull(middle_grad)
    branch_low = branch_grad.astype(bf_type)
    grad_out = jnp.einsum("tk,td->kd", mixed_low, branch_low, preferred_element_type=jnp.float32)
    mixed_grad = jnp.einsum(
        "td,kd->tk", branch_low, wo_full, preferred_element_type=jnp.float32
    ).astype(bf_type)
    grad_blocks = mixed_grad.reshape(blocks, block, HQ, HD)
    key_value_terms, query_grads = attend_backward(
        query_blocks, grad_blocks, index_blocks, position_blocks, totals, all_key_values
    )
    key_value_grad = deliver_rows(
        key_value_terms.astype(jnp.bfloat16).reshape(8, tokens, 2 * HD)
    )
    query_grad = query_grads.reshape(tokens, HQ, HD)
    proj_grad, grad_g_query, grad_g_key = heads_pull(
        (query_grad, key_value_grad[:, :HD], key_value_grad[:, HD:])
    )
    proj_low = proj_grad.astype(bf_type)
    grad_qkv = jnp.einsum("td,tc->dc", normed_low, proj_low, preferred_element_type=jnp.float32)
    normed_grad = jnp.einsum("tc,dc->td", proj_low, wq_full, preferred_element_type=jnp.float32)
    input_more, grad_g_attn = pre_pull(normed_grad)
    input_grad = input_first + input_more
    grad_gains = jnp.concatenate(
        [grad_g_attn, grad_g_post, grad_g_ffn, grad_g_out, grad_g_query, grad_g_key]
    )
    result = sum_grads(
        {
            "qkv": grad_qkv.astype(bf_type).reshape(4, 2, 80, 1536),
            "out": grad_out.astype(bf_type).reshape(4, 2, 128, 640),
            "gu": grad_gate_up.astype(bf_type).reshape(4, 2, 80, 4096),
            "down": grad_down.astype(bf_type).reshape(4, 2, 256, 640),
            "gain": spread_gains(grad_gains.reshape(4, 2, 384)),
        }
    )
    summed = tuple(result[t].astype(jnp.float32) for t in ("qkv", "out", "gu", "down")) + (
        packed_gains(result["gain"]),
    )
    params = (w_qkv, w_out, w_gate_up, w_down, gains)
    firsts = (first_qkv, first_out, first_gate_up, first_down, first_gains)
    seconds = (second_qkv, second_out, second_gate_up, second_down, second_gains)
    rates = (D ** (-0.5), (HQ * HD) ** (-0.5), D ** (-0.5), FF ** (-0.5), 0.8)
    decays = (0.01, 0.01, 0.01, 0.01, 0.0)
    updated = [
        adamw(params[idx], summed[idx], firsts[idx], seconds[idx], rates[idx], decays[idx])
        for idx in range(5)
    ]
    return (
        output,
        input_grad,
        updated[0][0],
        updated[1][0],
        updated[2][0],
        updated[3][0],
        updated[4][0],
        updated[0][1],
        updated[1][1],
        updated[2][1],
        updated[3][1],
        updated[4][1],
        updated[0][2],
        updated[1][2],
        updated[2][2],
        updated[3][2],
        updated[4][2],
    )


def solution(mesh):
    placed = (
        P(("dp", "opt"), None),
        P(("dp", "opt"), None),
        P(("dp", "opt")),
        P("opt", None),
        P("opt", None),
        P("opt", None),
        P("opt", None),
        P("opt"),
        P("opt", None),
        P("opt", None),
        P("opt", None),
        P("opt", None),
        P("opt"),
        P("opt", None),
        P("opt", None),
        P("opt", None),
        P("opt", None),
        P("opt"),
    )
    return jax.shard_map(
        local,
        mesh=mesh,
        in_specs=placed,
        out_specs=(
            P(("dp", "opt"), None),
            P(("dp", "opt"), None),
            P("opt", None),
            P("opt", None),
            P("opt", None),
            P("opt", None),
            P("opt"),
            P("opt", None),
            P("opt", None),
            P("opt", None),
            P("opt", None),
            P("opt"),
            P("opt", None),
            P("opt", None),
            P("opt", None),
            P("opt", None),
            P("opt"),
        ),
        check_vma=False,
    )
```

```python
import jax
import jax.numpy as jnp
from jax import lax
from jax.experimental import pallas as pl
from jax.experimental.pallas import tpu as pltpu
from jax.sharding import PartitionSpec as P

D = 640
HQ = 4
HD = 256
FF = 2048
STEP = 10


norm_epsilon = 1e-06


MESH = pl.DeviceIdType.MESH
TENSORS = {
    "qkv": dict(rows=80, cols=1536, dim=1, kind=jnp.bfloat16),
    "out": dict(rows=128, cols=640, dim=0, kind=jnp.bfloat16),
    "gu": dict(rows=80, cols=4096, dim=1, kind=jnp.bfloat16),
    "down": dict(rows=256, cols=640, dim=0, kind=jnp.bfloat16),
    "gain": dict(rows=32, cols=128, dim=0, kind=jnp.float32),
}


class Place:
    def __init__(self):
        dp, opt = lax.axis_index("dp"), lax.axis_index("opt")
        self.xl, self.y, self.c = dp // 8, (dp // 2) % 4, dp % 2
        self.z, self.xh = opt // 2, opt % 2
        self.x = self.xh * 2 + self.xl

    def device(self, xl=None, y=None, c=None, z=None, xh=None):
        xl = self.xl if xl is None else xl
        y = self.y if y is None else y
        c = self.c if c is None else c
        z = self.z if z is None else z
        xh = self.xh if xh is None else xh
        return ((xl * 4 + y) * 2 + c, z * 2 + xh)

    def on_z(self, k):
        z = (self.z + k) % 4
        return z, self.device(z=z)

    def on_y(self, k):
        y = (self.y + k) % 4
        return y, self.device(y=y)

    def on_x(self, k):
        x = (self.x + k) % 4
        return (x // 2, x % 2), self.device(xh=x // 2, xl=x % 2)

    def other_core(self):
        return self.device(c=1 - self.c)

    def pair(self):
        return self.device(xl=1 - self.xl)


def greet(devices):
    barrier = pltpu.get_barrier_semaphore()
    for device in devices:
        pl.semaphore_signal(barrier, inc=1, device_id=device, device_id_type=MESH)
    pl.semaphore_wait(barrier, len(devices))


def cut(ref, name, lead, start, size):
    dim = TENSORS[name]["dim"]
    if isinstance(start, int):
        window = pl.ds(start, size)
    else:
        window = pl.ds(pl.multiple_of(start, 128 if dim else (16 if name != "gain" else 8)), size)
    if dim:
        return ref.at[(*lead, slice(None), window)]
    return ref.at[(*lead, window)]


class Copies:
    def __init__(self, send, recv):
        self.send, self.recv, self.used = send, recv, 0

    def remote(self, src, dst, device):
        i = self.used
        self.used += 1
        copy = pltpu.make_async_remote_copy(
            src_ref=src,
            dst_ref=dst,
            send_sem=self.send.at[i],
            recv_sem=self.recv.at[i],
            device_id=device,
            device_id_type=MESH,
        )
        copy.start()
        return copy

    def here(self, src, dst):
        i = self.used
        self.used += 1
        copy = pltpu.make_async_copy(src, dst, self.send.at[i])
        copy.start()
        return copy


GATHER = ("qkv", "gain", "out", "gu", "down")
ORDER = {"qkv": "xz", "gain": "xz", "out": "xz", "down": "zx", "gu": "zxy"}
K3 = (1, 2, 3)


def gather_steps(at, copies, name, shard, full):
    spec = TENSORS[name]
    unit = spec["rows" if spec["dim"] == 0 else "cols"] // 4
    every = slice(None)
    z, xh, xl, y, c = at.z, at.xh, at.xl, at.y, at.c
    order = ORDER[name]
    started = []

    def send(view, device):
        started.append(copies.remote(view, view, device))
        return started[-1]

    if order == "zxy":
        sub = unit // 4
        own = c * (8 * sub) + y * (2 * sub) + xl * sub
        size = sub
    else:
        own = (c * 2 + xl) * unit
        size = unit
    mine = cut(shard, name, (), own, size)
    here = copies.here(mine, cut(full, name, (z, xh), own, size))
    land = cut(full, name, (z, xh), own, size)
    first = []
    for k in K3:
        device = at.on_x(k)[1] if order == "xz" else at.on_z(k)[1]
        first.append(copies.remote(mine, land, device))
    started.extend(first)
    yield
    here.wait()
    for copy in first:
        copy.wait_recv()
    if order == "xz":
        view = cut(full, name, (z, every), c * 2 * unit, 2 * unit)
        second = [send(view, at.on_z(k)[1]) for k in K3]
        last = [send(view, at.other_core())]
        yield
        for copy, k in zip(second, K3):
            copy.wait_recv()
            zz = (z - k) % 4
            last.append(send(cut(full, name, (zz, every), c * 2 * unit, 2 * unit), at.other_core()))
    elif order == "zx":
        view = cut(full, name, (every, xh), own, size)
        second = [send(view, at.on_x(k)[1]) for k in K3]
        last = [send(view, at.other_core())]
        yield
        for copy, k in zip(second, K3):
            copy.wait_recv()
            xx = (at.x - k) % 4
            view = cut(full, name, (every, xx // 2), (c * 2 + xx % 2) * unit, size)
            last.append(send(view, at.other_core()))
    else:
        view = cut(full, name, (every, xh), own, size)
        second = [send(view, at.on_x(k)[1]) for k in K3]
        yield
        for copy in second:
            copy.wait_recv()
        wide = 2 * sub
        view = cut(full, name, (every, every), c * (8 * sub) + y * wide, wide)
        third = [send(view, at.on_y(k)[1]) for k in K3]
        last = [send(view, at.other_core())]
        yield
        for copy, k in zip(third, K3):
            copy.wait_recv()
            yy = (y - k) % 4
            view = cut(full, name, (every, every), c * (8 * sub) + yy * wide, wide)
            last.append(send(view, at.other_core()))
    yield
    for copy in last:
        copy.wait_recv()
    for copy in started:
        copy.wait_send()


def run_all(steps):
    steps = list(steps)
    while steps:
        left = []
        for step in steps:
            try:
                next(step)
                left.append(step)
            except StopIteration:
                pass
        steps = left


def everyone(at):
    found = [at.other_core()]
    for k in K3:
        found += [at.on_z(k)[1], at.on_x(k)[1], at.on_y(k)[1]]
    return found


SUM = ("gu", "down", "out", "qkv", "gain")
SUM_ORDER = {"qkv": "zxy", "gain": "zxy", "out": "zxy", "down": "xzy", "gu": "yxz"}


def shaped(name, lead, split):
    spec = TENSORS[name]
    rows, cols = spec["rows"], spec["cols"]
    if spec["dim"]:
        return (*lead, rows, cols // split)
    return (*lead, rows // split, cols)


def sum_scratch(name):
    kind = TENSORS[name]["kind"]
    order = SUM_ORDER[name]
    if order == "zxy":
        shapes = [((4, 2), 2), ((3, 2), 2), ((2,), 2), ((3,), 4), ((), 4), ((3,), 4)]
    elif order == "xzy":
        shapes = [((4, 2), 2), ((3, 4), 4), ((4,), 4), ((3,), 4), ((), 4), ((3,), 4)]
    else:
        shapes = [((4, 2), 2), ((3, 4, 2), 8), ((4, 2), 8), ((3, 4), 16), ((4,), 16), ((3,), 16)]
    return [pltpu.VMEM(shaped(name, lead, split), kind) for lead, split in shapes]


def sum_steps(at, copies, name, grad, result, landed, land1, sum1, land2, sum2, land3):
    spec = TENSORS[name]
    order = SUM_ORDER[name]
    kind = spec["kind"]
    unit = spec["rows" if spec["dim"] == 0 else "cols"] // 4
    half = 2 * unit
    every = slice(None)
    z, xh, xl, y, c = at.z, at.xh, at.xl, at.y, at.c
    f32 = jnp.float32
    started = []

    def send(src, dst, device):
        started.append(copies.remote(src, dst, device))
        return started[-1]

    def add(own, arrived, target):
        value = own[...].astype(f32)
        for ref in arrived:
            value = value + ref[...].astype(f32)
        target[...] = value.astype(kind)

    swap = send(cut(grad, name, (every, every), (1 - c) * half, half), landed, at.other_core())
    yield
    swap.wait_recv()

    def joined(i, carry):
        a, b = i // 2, i % 2
        add(cut(grad, name, (a, b), c * half, half), [landed.at[a, b]], landed.at[a, b])
        return carry

    lax.fori_loop(0, 8, joined, 0)
    if order == "zxy":
        first = [send(landed.at[at.on_z(k)[0]], land1.at[k - 1], at.on_z(k)[1]) for k in K3]
        yield
        for copy in first:
            copy.wait_recv()
        for b in range(2):
            add(landed.at[z, b], [land1.at[i, b] for i in range(3)], sum1.at[b])
        second = []
        for k in K3:
            (xxh, xxl), device = at.on_x(k)
            second.append(send(cut(sum1, name, (xxh,), xxl * unit, unit), land2.at[k - 1], device))
        yield
        for copy in second:
            copy.wait_recv()
        add(cut(sum1, name, (xh,), xl * unit, unit), [land2.at[i] for i in range(3)], sum2)
    elif order == "xzy":
        first = []
        for k in K3:
            (xxh, xxl), device = at.on_x(k)
            first.append(
                send(cut(landed, name, (every, xxh), xxl * unit, unit), land1.at[k - 1], device)
            )
        yield
        for copy in first:
            copy.wait_recv()
        for a in range(4):
            add(
                cut(landed, name, (a, xh), xl * unit, unit),
                [land1.at[i, a] for i in range(3)],
                sum1.at[a],
            )
        second = [send(sum1.at[at.on_z(k)[0]], land2.at[k - 1], at.on_z(k)[1]) for k in K3]
        yield
        for copy in second:
            copy.wait_recv()
        add(sum1.at[z], [land2.at[i] for i in range(3)], sum2)
    else:
        sub = unit // 4
        first = []
        for k in K3:
            yy, device = at.on_y(k)
            first.append(
                send(cut(landed, name, (every, every), yy * 2 * sub, 2 * sub), land1.at[k - 1], device)
            )
        yield
        for copy in first:
            copy.wait_recv()

        def over(i, carry):
            a, b = i // 2, i % 2
            add(
                cut(landed, name, (a, b), y * 2 * sub, 2 * sub),
                [land1.at[j, a, b] for j in range(3)],
                sum1.at[a, b],
            )
            return carry

        lax.fori_loop(0, 8, over, 0)
        second = []
        for k in K3:
            (xxh, xxl), device = at.on_x(k)
            second.append(send(cut(sum1, name, (every, xxh), xxl * sub, sub), land2.at[k - 1], device))
        yield
        for copy in second:
            copy.wait_recv()
        for a in range(4):
            add(
                cut(sum1, name, (a, xh), xl * sub, sub),
                [land2.at[i, a] for i in range(3)],
                sum2.at[a],
            )
        third = [send(sum2.at[at.on_z(k)[0]], land3.at[k - 1], at.on_z(k)[1]) for k in K3]
        yield
        for copy in third:
            copy.wait_recv()
        place = c * (8 * sub) + y * (2 * sub) + xl * sub
        mine = cut(result, name, (), place, sub)
        add(sum2.at[z], [land3.at[i] for i in range(3)], mine)
        near = send(mine, mine, at.pair())
        yield
        near.wait_recv()
        wide = cut(result, name, (), c * (8 * sub) + y * (2 * sub), 2 * sub)
        around = [send(wide, wide, at.on_y(k)[1]) for k in K3]
        yield
        for copy in around:
            copy.wait_recv()
    if order != "yxz":
        third = [send(sum2, land3.at[k - 1], at.on_y(k)[1]) for k in K3]
        yield
        for copy in third:
            copy.wait_recv()
        mine = cut(result, name, (), (c * 2 + xl) * unit, unit)
        add(sum2, [land3.at[i] for i in range(3)], mine)
        near = send(mine, mine, at.pair())
        yield
        near.wait_recv()
    whole = cut(result, name, (), c * half, half)
    across = send(whole, whole, at.other_core())
    yield
    across.wait_recv()
    for copy in started:
        copy.wait_send()


def spread_gains(values):
    lead = values.shape[:-1]
    rows = values.reshape(*lead, 3, 1, 128)
    rows = jnp.pad(rows, [(0, 0)] * len(lead) + [(0, 1), (0, 7), (0, 0)])
    return rows.reshape(*lead, 32, 128)


def packed_gains(rows):
    lead = rows.shape[:-2]
    return rows.reshape(*lead, 4, 8, 128)[..., :3, 0, :].reshape(*lead, 384)


def rotary_tables(positions):
    freqs = 1000000.0 ** (-(jnp.arange(HD // 2, dtype=jnp.float32) * 2.0 / HD))
    angles = positions.astype(jnp.float32)[:, None] * freqs[None, :]
    return (jnp.cos(angles), jnp.sin(angles))


NN = (((1,), (0,)), ((), ()))
NT = (((1,), (1,)), ((), ()))
TN = (((0,), (0,)), ((), ()))
WIDE = 512
F32 = jnp.float32
LOW = jnp.bfloat16


def mul(left, right, dims=NN):
    return lax.dot_general(left, right, dims, preferred_element_type=F32)


def inverse_rms(values):
    return lax.rsqrt(jnp.mean(values * values, axis=-1, keepdims=True) + norm_epsilon)


def norm_back(grad, hat, inverse, gain):
    scaled = grad * gain
    inner = jnp.mean(scaled * hat, axis=-1, keepdims=True)
    return jnp.sum(grad * hat, axis=0, keepdims=True), (scaled - hat * inner) * inverse


def turn(values, cosine, sine):
    half = values.shape[-1] // 2
    u, w = values[:, :half], values[:, half:]
    return jnp.concatenate([u * cosine - w * sine, w * cosine + u * sine], axis=1)


def gain_row(gain_ref, first, count):
    pieces = []
    for chunk in range(first, first + count):
        opt, row = chunk // 3, (chunk % 3) * 8
        pieces.append(gain_ref[opt // 2, opt % 2, row : row + 1, :])
    return jnp.concatenate(pieces, axis=1)


def put_gain(gain_ref, first, count, row_values):
    for i in range(count):
        chunk = first + i
        opt, row = chunk // 3, (chunk % 3) * 8
        gain_ref[opt // 2, opt % 2, row : row + 1, :] = row_values[:, i * 128 : (i + 1) * 128]


def step_kernel(*refs):
    x, ct, cosine, sine, pos = refs[:5]
    shards = dict(zip(GATHER, refs[5:10]))
    out, in_grad = refs[10:12]
    results = dict(zip(SUM, refs[12:17]))
    rest = list(refs[17:])

    def take(n):
        taken = rest[:n]
        del rest[:n]
        return taken

    weights = dict(zip(GATHER, take(5)))
    grads = dict(zip(SUM, take(5)))
    landing = {name: take(6) for name in SUM}
    qkv, q_b, kv_all, o_acc, l_sum, o_b = take(6)
    branch, middle, gate, up, hidden, ffn, normed, down = take(8)
    do_b, dq, dkv, parts, landed, d_mid, d_ffn, dqkv = take(8)
    send, recv, kv_send, kv_recv, dkv_send, dkv_recv = take(6)
    at = Place()
    me = at.z * 2 + at.xh
    peers = everyone(at) + [at.device(z=at.on_z(k)[0], xh=1 - at.xh) for k in K3]
    greet(peers)
    copies = Copies(send, recv)
    fetch = {t: gather_steps(at, copies, t, shards[t], weights[t]) for t in GATHER}

    def go(steps):
        next(steps, None)

    def member(opt):
        return at.device(z=opt // 2, xh=opt % 2)

    go(fetch["qkv"])
    go(fetch["gain"])
    xs = x[...]
    inv_x = inverse_rms(xs)
    x_hat = xs * inv_x
    go(fetch["qkv"])
    go(fetch["gain"])
    go(fetch["gu"])
    go(fetch["down"])
    go(fetch["out"])
    go(fetch["qkv"])
    go(fetch["gain"])
    go(fetch["gain"])
    gain = weights["gain"]
    normed[...] = (x_hat * gain_row(gain, 0, 5)).astype(LOW)
    go(fetch["qkv"])
    w_qkv, w_out, w_gu, w_down = (weights[t] for t in ("qkv", "out", "gu", "down"))

    low_in = normed[...]
    kv_cols = mul(low_in, w_qkv[:, :, :, 1024:1536].reshape(D, 512))
    qkv[:, 1024:1536] = kv_cols
    keys = kv_cols[:, :HD]
    k_low = turn(keys * inverse_rms(keys) * gain_row(gain, 22, 2), cosine[...], sine[...]).astype(LOW)
    kv_all[me] = jnp.concatenate([k_low, kv_cols[:, HD:].astype(LOW)], axis=1)

    def kv_copy(k, slot, opt):
        return pltpu.make_async_remote_copy(
            src_ref=kv_all.at[slot],
            dst_ref=kv_all.at[slot],
            send_sem=kv_send.at[k],
            recv_sem=kv_recv.at[k],
            device_id=member(opt),
            device_id_type=MESH,
        )

    for k in range(1, 8):

        @pl.when(me + k < 8)
        def _():
            kv_copy(k, me, me + k).start()

    go(fetch["gu"])
    go(fetch["down"])
    go(fetch["out"])
    g_query = gain_row(gain, 20, 2)
    for part in range(2):
        cols = mul(low_in, w_qkv[:, :, :, part * 512 : part * 512 + 512].reshape(D, 512))
        qkv[:, part * 512 : part * 512 + 512] = cols
        for i in range(2):
            q = cols[:, i * HD : (i + 1) * HD]
            q = turn(q * inverse_rms(q) * g_query, cosine[...], sine[...]).astype(LOW)
            q_b[part * 2 + i] = q * jnp.asarray(HD**-0.5, LOW)

    o_acc[...] = jnp.zeros_like(o_acc)
    l_sum[...] = jnp.zeros_like(l_sum)
    tokens = x.shape[0]
    shift = lax.broadcasted_iota(jnp.int32, (tokens, tokens), 0) - lax.broadcasted_iota(
        jnp.int32, (tokens, tokens), 1
    )

    def allowed(k):
        offset = shift + k * tokens
        return (offset >= 0) & (offset <= pos[...])

    def forward_block(k, carry):
        @pl.when(k > 0)
        def _():
            kv_copy(k, me - k, me - k).wait_recv()

        kv = kv_all[me - k]
        ok = allowed(k)
        for h in range(HQ):
            s = mul(q_b[h], kv[:, :HD], NT)
            e = jnp.where(ok, jnp.exp(s), 0.0)
            l_sum[h] += e[:, :128] + e[:, 128:]
            o_acc[h] += mul(e.astype(LOW), kv[:, HD:])
        return carry

    def blocks(body, low_k, high_k):
        lax.fori_loop(low_k, jnp.minimum(me + 1, high_k), body, 0)

    blocks(forward_block, 0, 1)
    go(fetch["gu"])
    go(fetch["down"])
    go(fetch["out"])
    blocks(forward_block, 1, 8)
    for h in range(HQ):
        l_inv = 1.0 / jnp.sum(l_sum[h], axis=-1, keepdims=True)
        o = o_acc[h] * l_inv
        o_acc[h] = o
        l_sum[h] = jnp.broadcast_to(l_inv, (tokens, 128))
        o_b[:, h * HD : (h + 1) * HD] = o.astype(LOW)
    go(fetch["out"])
    r = mul(o_b[...], w_out[...].reshape(HQ * HD, D))
    branch[...] = r
    x1 = x[...] + r * inverse_rms(r) * gain_row(gain, 5, 5)
    middle[...] = x1
    ffn[...] = (x1 * inverse_rms(x1) * gain_row(gain, 10, 5)).astype(LOW)
    go(fetch["gu"])
    go(fetch["down"])
    go(fetch["gu"])

    root = 0.7978845608028654

    def up_chunk(i, carry):
        cols = pl.ds(pl.multiple_of(i * WIDE, WIDE), WIDE)
        more = pl.ds(pl.multiple_of(FF + i * WIDE, WIDE), WIDE)
        b = ffn[...]
        z = mul(b, w_gu[:, :, :, cols].reshape(D, WIDE))
        u = mul(b, w_gu[:, :, :, more].reshape(D, WIDE))
        t = jnp.tanh(root * (z + 0.044715 * z * z * z))
        gelu = 0.5 * z * (1.0 + t)
        slope = 0.5 * (1.0 + t) + 0.5 * z * (1.0 - t * t) * root * (1.0 + 3.0 * 0.044715 * z * z)
        gate[:, cols] = slope * u
        up[:, cols] = gelu
        hidden[:, cols] = (gelu * u).astype(LOW)
        return carry

    lax.fori_loop(0, FF // WIDE, up_chunk, 0)
    m = mul(hidden[...], w_down[...].reshape(FF, D))
    inv_m = inverse_rms(m)
    m_hat = m * inv_m
    g_out = gain_row(gain, 15, 5)
    out[...] = middle[...] + m_hat * g_out
    total = {t: sum_steps(at, copies, t, grads[t], results[t], *landing[t]) for t in SUM}
    grad_gain = grads["gain"]
    grad_gain[...] = jnp.zeros_like(grad_gain)
    grad_row, dm = norm_back(ct[...], m_hat, inv_m, g_out)
    put_gain(grad_gain, 15, 5, grad_row)
    down[...] = dm.astype(LOW)

    d_ffn[...] = jnp.zeros_like(d_ffn)

    def down_chunk(i, carry):
        cols = pl.ds(pl.multiple_of(i * WIDE, WIDE), WIDE)
        more = pl.ds(pl.multiple_of(FF + i * WIDE, WIDE), WIDE)
        dm_b, b = down[...], ffn[...]
        dh = mul(dm_b, w_down[i].reshape(WIDE, D), NT)
        d_gate = (dh * gate[:, cols]).astype(LOW)
        d_up = (dh * up[:, cols]).astype(LOW)
        grads["gu"][:, :, :, cols] = mul(b, d_gate, TN).astype(LOW).reshape(4, 2, 80, WIDE)
        grads["gu"][:, :, :, more] = mul(b, d_up, TN).astype(LOW).reshape(4, 2, 80, WIDE)
        grads["down"][i] = mul(hidden[:, cols], dm_b, TN).astype(LOW).reshape(2, 256, D)
        d_ffn[...] += mul(d_gate, w_gu[:, :, :, cols].reshape(D, WIDE), NT) + mul(
            d_up, w_gu[:, :, :, more].reshape(D, WIDE), NT
        )
        return carry

    lax.fori_loop(0, FF // WIDE, down_chunk, 0)
    go(total["gu"])
    go(total["down"])
    x1 = middle[...]
    inv_1 = inverse_rms(x1)
    grad_row, dx = norm_back(d_ffn[...], x1 * inv_1, inv_1, gain_row(gain, 10, 5))
    put_gain(grad_gain, 10, 5, grad_row)
    dx = ct[...] + dx
    d_mid[...] = dx
    r = branch[...]
    inv_r = inverse_rms(r)
    grad_row, dr = norm_back(dx, r * inv_r, inv_r, gain_row(gain, 5, 5))
    put_gain(grad_gain, 5, 5, grad_row)
    dr_b = dr.astype(LOW)
    go(total["gu"])
    for h in range(HQ):
        grads["out"][h] = mul(o_b[:, h * HD : (h + 1) * HD], dr_b, TN).astype(LOW).reshape(2, 128, D)
        do_b[h] = mul(dr_b, w_out[h].reshape(HD, D), NT).astype(LOW)
    go(total["out"])
    go(total["down"])
    for h in range(HQ):
        delta = jnp.sum(o_acc[h] * do_b[h].astype(F32), axis=-1, keepdims=True)
        o_acc[h, :, :128] = jnp.broadcast_to(delta, (tokens, 128))
    go(total["out"])
    dq[...] = jnp.zeros_like(dq)

    def back_block(k):
        kv = kv_all[me - k]
        keys, values = kv[:, :HD], kv[:, HD:]
        ok = allowed(k)
        d_keys = d_values = None
        for h in range(HQ):
            s = mul(q_b[h], keys, NT)
            p = jnp.where(ok, jnp.exp(s) * l_sum[h, :, :1], 0.0)
            dp = mul(do_b[h], values, NT)
            ds = (p * (dp - o_acc[h, :, :1])).astype(LOW)
            dq[h] += mul(ds, keys)
            more_keys = mul(ds, q_b[h], TN)
            more_values = mul(p.astype(LOW), do_b[h], TN)
            d_keys = more_keys if h == 0 else d_keys + more_keys
            d_values = more_values if h == 0 else d_values + more_values
        return d_keys, d_values

    def dkv_copy(k, opt):
        return pltpu.make_async_remote_copy(
            src_ref=parts.at[k - 1],
            dst_ref=landed.at[k - 1],
            send_sem=dkv_send.at[k],
            recv_sem=dkv_recv.at[k],
            device_id=member(opt),
            device_id_type=MESH,
        )

    def away_block(k, carry):
        d_keys, d_values = back_block(k)
        parts[k - 1, :, :HD] = d_keys.astype(LOW)
        parts[k - 1, :, HD:] = d_values.astype(LOW)
        dkv_copy(k, me - k).start()
        return carry

    blocks(away_block, 1, 4)
    go(total["down"])
    go(total["out"])
    blocks(away_block, 4, 8)
    d_keys, d_values = back_block(0)
    dkv[:, :HD] = d_keys
    dkv[:, HD:] = d_values
    go(total["gu"])
    go(total["down"])
    go(total["out"])

    grad_row = None
    for h in range(HQ):
        q = qkv[:, h * HD : (h + 1) * HD]
        inv_q = inverse_rms(q)
        e = turn(dq[h] * HD**-0.5, cosine[...], -sine[...])
        more, back = norm_back(e, q * inv_q, inv_q, g_query)
        grad_row = more if h == 0 else grad_row + more
        dqkv[:, h * HD : (h + 1) * HD] = back.astype(LOW)
    put_gain(grad_gain, 20, 2, grad_row)
    low_in = normed[...]
    for part in range(2):
        cols = slice(part * 512, part * 512 + 512)
        grads["qkv"][:, :, :, cols] = mul(low_in, dqkv[:, cols], TN).astype(LOW).reshape(4, 2, 80, 512)

    def arrived(k, carry):
        dkv_copy(k, me - k + 8).wait_recv()
        dkv[...] += landed[k - 1].astype(F32)
        return carry

    lax.fori_loop(1, 8 - me, arrived, 0)
    keys = qkv[:, 1024:1280]
    inv_k = inverse_rms(keys)
    e = turn(dkv[:, :HD], cosine[...], -sine[...])
    grad_row, back = norm_back(e, keys * inv_k, inv_k, gain_row(gain, 22, 2))
    put_gain(grad_gain, 22, 2, grad_row)
    dqkv[:, 1024:1280] = back.astype(LOW)
    dqkv[:, 1280:1536] = dkv[:, HD:].astype(LOW)
    grads["qkv"][:, :, :, 1024:1536] = (
        mul(low_in, dqkv[:, 1024:1536], TN).astype(LOW).reshape(4, 2, 80, 512)
    )
    go(total["qkv"])
    d_normed = mul(dqkv[...], w_qkv[...].reshape(D, 1536), NT)
    xs = x[...]
    inv_x = inverse_rms(xs)
    grad_row, back = norm_back(d_normed, xs * inv_x, inv_x, gain_row(gain, 0, 5))
    put_gain(grad_gain, 0, 5, grad_row)
    go(total["gain"])
    in_grad[...] = d_mid[...] + back
    go(total["qkv"])
    go(total["gain"])
    for k in range(1, 8):

        @pl.when(me + k < 8)
        def _():
            kv_copy(k, me, me + k).wait_send()

        @pl.when(me - k >= 0)
        def _():
            dkv_copy(k, me - k).wait_send()

    run_all(
        [
            fetch["out"],
            fetch["down"],
            fetch["gu"],
            total["qkv"],
            total["gain"],
            total["gu"],
            total["down"],
            total["out"],
        ]
    )


def one_step(inputs, cotangent, cosine, sine, positions, shards):
    vmem = pl.BlockSpec(memory_space=pltpu.VMEM)
    hbm = pl.BlockSpec(memory_space=pltpu.HBM)
    tokens = inputs.shape[0]

    def full(t):
        return pltpu.VMEM((4, 2, TENSORS[t]["rows"], TENSORS[t]["cols"]), TENSORS[t]["kind"])

    scratch = [full(t) for t in GATHER] + [full(t) for t in SUM]
    for t in SUM:
        scratch += sum_scratch(t)
    scratch += [
        pltpu.VMEM((tokens, 1536), F32),
        pltpu.VMEM((HQ, tokens, HD), LOW),
        pltpu.VMEM((8, tokens, 2 * HD), LOW),
        pltpu.VMEM((HQ, tokens, HD), F32),
        pltpu.VMEM((HQ, tokens, 128), F32),
        pltpu.VMEM((tokens, HQ * HD), LOW),
        pltpu.VMEM((tokens, D), F32),
        pltpu.VMEM((tokens, D), F32),
        pltpu.VMEM((tokens, FF), F32),
        pltpu.VMEM((tokens, FF), F32),
        pltpu.VMEM((tokens, FF), LOW),
        pltpu.VMEM((tokens, D), LOW),
        pltpu.VMEM((tokens, D), LOW),
        pltpu.VMEM((tokens, D), LOW),
        pltpu.VMEM((HQ, tokens, HD), LOW),
        pltpu.VMEM((HQ, tokens, HD), F32),
        pltpu.VMEM((tokens, 2 * HD), F32),
        pltpu.VMEM((7, tokens, 2 * HD), LOW),
        pltpu.VMEM((7, tokens, 2 * HD), LOW),
        pltpu.VMEM((tokens, D), F32),
        pltpu.VMEM((tokens, D), F32),
        pltpu.VMEM((tokens, 1536), LOW),
        pltpu.SemaphoreType.DMA((160,)),
        pltpu.SemaphoreType.DMA((160,)),
    ] + [pltpu.SemaphoreType.DMA((8,))] * 4
    outs = pl.pallas_call(
        step_kernel,
        name="one_step",
        out_shape=[jax.ShapeDtypeStruct((tokens, D), F32)] * 2
        + [
            jax.ShapeDtypeStruct((TENSORS[t]["rows"], TENSORS[t]["cols"]), TENSORS[t]["kind"])
            for t in SUM
        ],
        in_specs=[vmem] * 5 + [hbm] * 5,
        out_specs=[vmem] * 7,
        scratch_shapes=scratch,
        compiler_params=pltpu.CompilerParams(
            collective_id=1, has_side_effects=True, vmem_limit_bytes=62 * 2**20
        ),
    )(inputs, cotangent, cosine, sine, positions, *[shards[t] for t in GATHER])
    return outs[0], outs[1], dict(zip(SUM, outs[2:]))


def adamw(weight, gradient, first, second, step_rate, weight_decay):
    new_first = 0.9 * first + 0.1 * gradient
    new_second = 0.999 * second + 0.001 * gradient * gradient
    first_hat = new_first / (1.0 - 0.9**STEP)
    second_hat = new_second / (1.0 - 0.999**STEP)
    new_weight = weight - step_rate * (
        first_hat / (jnp.sqrt(second_hat) + 1e-08) + weight_decay * weight
    )
    return (new_weight, new_first, new_second)


def local(
    inputs,
    cotangent,
    positions,
    w_qkv,
    w_out,
    w_gate_up,
    w_down,
    gains,
    first_qkv,
    first_out,
    first_gate_up,
    first_down,
    first_gains,
    second_qkv,
    second_out,
    second_gate_up,
    second_down,
    second_gains,
):
    cosine, sine = rotary_tables(positions)
    output, input_grad, result = one_step(
        inputs,
        cotangent,
        cosine,
        sine,
        positions[:, None],
        {
            "qkv": w_qkv.astype(LOW),
            "out": w_out.astype(LOW),
            "gu": w_gate_up.astype(LOW),
            "down": w_down.astype(LOW),
            "gain": spread_gains(gains.astype(LOW).astype(F32)),
        },
    )
    summed = tuple(result[t].astype(F32) for t in ("qkv", "out", "gu", "down")) + (
        packed_gains(result["gain"]),
    )
    params = (w_qkv, w_out, w_gate_up, w_down, gains)
    firsts = (first_qkv, first_out, first_gate_up, first_down, first_gains)
    seconds = (second_qkv, second_out, second_gate_up, second_down, second_gains)
    rates = (D ** (-0.5), (HQ * HD) ** (-0.5), D ** (-0.5), FF ** (-0.5), 0.8)
    decays = (0.01, 0.01, 0.01, 0.01, 0.0)
    updated = [
        adamw(params[idx], summed[idx], firsts[idx], seconds[idx], rates[idx], decays[idx])
        for idx in range(5)
    ]
    return (
        output,
        input_grad,
        updated[0][0],
        updated[1][0],
        updated[2][0],
        updated[3][0],
        updated[4][0],
        updated[0][1],
        updated[1][1],
        updated[2][1],
        updated[3][1],
        updated[4][1],
        updated[0][2],
        updated[1][2],
        updated[2][2],
        updated[3][2],
        updated[4][2],
    )


def solution(mesh):
    placed = (
        P(("dp", "opt"), None),
        P(("dp", "opt"), None),
        P(("dp", "opt")),
        P("opt", None),
        P("opt", None),
        P("opt", None),
        P("opt", None),
        P("opt"),
        P("opt", None),
        P("opt", None),
        P("opt", None),
        P("opt", None),
        P("opt"),
        P("opt", None),
        P("opt", None),
        P("opt", None),
        P("opt", None),
        P("opt"),
    )
    return jax.shard_map(
        local,
        mesh=mesh,
        in_specs=placed,
        out_specs=(
            P(("dp", "opt"), None),
            P(("dp", "opt"), None),
            P("opt", None),
            P("opt", None),
            P("opt", None),
            P("opt", None),
            P("opt"),
            P("opt", None),
            P("opt", None),
            P("opt", None),
            P("opt", None),
            P("opt"),
            P("opt", None),
            P("opt", None),
            P("opt", None),
            P("opt", None),
            P("opt"),
        ),
        check_vma=False,
    )
```

```python
import jax
import jax.numpy as jnp
from jax import lax
from jax.experimental import pallas as pl
from jax.experimental.pallas import tpu as pltpu
from jax.sharding import PartitionSpec as P

D = 640
HQ = 4
HD = 256
FF = 2048
STEP = 10


norm_epsilon = 1e-06


MESH = pl.DeviceIdType.MESH
F32 = jnp.float32
LOW = jnp.bfloat16
K3 = (1, 2, 3)
EVERY = slice(None)
ARRAYS = {
    "qkv": (80, 1536, LOW),
    "gain": (32, 128, F32),
    "out": (128, 640, LOW),
    "gu": (80, 4096, LOW),
    "down": (256, 640, LOW),
}
PIECES = {
    "kv": ("qkv", 1, 1024, 512),
    "q": ("qkv", 1, 0, 1024),
    "gain": ("gain", 0, 0, 32),
    "out": ("out", 0, 0, 128),
    "gate": ("gu", 1, 0, 2048),
    "up": ("gu", 1, 2048, 2048),
    "down": ("down", 0, 0, 256),
}


class Place:
    def __init__(self):
        dp, opt = lax.axis_index("dp"), lax.axis_index("opt")
        self.xl, self.y, self.c = dp // 8, (dp // 2) % 4, dp % 2
        self.z, self.xh = opt // 2, opt % 2
        self.x = self.xh * 2 + self.xl

    def device(self, xl=None, y=None, c=None, z=None, xh=None):
        xl = self.xl if xl is None else xl
        y = self.y if y is None else y
        c = self.c if c is None else c
        z = self.z if z is None else z
        xh = self.xh if xh is None else xh
        return ((xl * 4 + y) * 2 + c, z * 2 + xh)

    def on_z(self, k):
        return self.device(z=(self.z + k) % 4)

    def on_y(self, k):
        return self.device(y=(self.y + k) % 4)

    def on_x(self, k):
        x = (self.x + k) % 4
        return self.device(xh=x // 2, xl=x % 2)

    def on_plane(self, i, k):
        x = (self.x + k) % 4
        return self.device(z=(self.z + i) % 4, xh=x // 2, xl=x % 2)

    def other_core(self):
        return self.device(c=1 - self.c)

    def pair(self):
        return self.device(xl=1 - self.xl)

    def across(self):
        return self.device(xl=1 - self.xl, c=1 - self.c)

    def facing(self, i):
        return self.device(z=(self.z + i) % 4, xh=1 - self.xh, xl=1 - self.xl)


PLANE = [(i, k) for i in range(4) for k in range(4) if i or k]


def everyone(at):
    found = [at.other_core(), at.across()]
    found += [at.on_y(k) for k in K3]
    found += [at.on_plane(i, k) for i, k in PLANE]
    return found


def greet(devices):
    barrier = pltpu.get_barrier_semaphore()
    for device in devices:
        pl.semaphore_signal(barrier, inc=1, device_id=device, device_id_type=MESH)
    pl.semaphore_wait(barrier, len(devices))


def window(dim, start, size, grain):
    part = pl.ds(start if isinstance(start, int) else pl.multiple_of(start, grain), size)
    return (EVERY, part) if dim else (part, EVERY)


class Piece:
    def __init__(self, name):
        self.array, self.dim, self.base, self.extent = PIECES[name]
        self.rows, self.cols, self.kind = ARRAYS[self.array]
        self.grain = 128 if self.dim else (8 if self.kind == F32 else 16)

    def of(self, ref, lead, start, size):
        return ref.at[(*lead, *window(self.dim, self.base + start, size, self.grain))]

    def within(self, ref, lead, start, size):
        return ref.at[(*lead, *window(self.dim, start, size, self.grain))]

    def buffer(self, lead, part):
        size = self.extent // part
        shape = (self.rows, size) if self.dim else (size, self.cols)
        return pltpu.VMEM((*lead, *shape), self.kind)


class Copies:
    def __init__(self, send, recv):
        self.send, self.recv, self.used = send, recv, 0

    def remote(self, src, dst, device):
        i = self.used
        self.used += 1
        copy = pltpu.make_async_remote_copy(
            src_ref=src,
            dst_ref=dst,
            send_sem=self.send.at[i],
            recv_sem=self.recv.at[i],
            device_id=device,
            device_id_type=MESH,
        )
        copy.start()
        return copy

    def here(self, src, dst):
        i = self.used
        self.used += 1
        copy = pltpu.make_async_copy(src, dst, self.send.at[i])
        copy.start()
        return copy


GATHER_PLAN = {
    "kv": "plane",
    "gain": "plane",
    "q": "facing y",
    "gate": "z x y",
    "down": "x z y",
    "up": "z x",
    "out": "x z",
}


def gather_steps(at, copies, name, shard, full):
    piece = Piece(name)
    plan = GATHER_PLAN[name]
    n = piece.extent
    z, xh, xl, y, c = at.z, at.xh, at.xl, at.y, at.c
    started, swaps = [], []

    def send(view, device):
        started.append(copies.remote(view, view, device))
        return started[-1]

    def swap(view):
        swaps.append(send(view, at.other_core()))

    if plan == "facing y":
        own, size = c * (n // 2) + y * (n // 8), n // 8
    elif plan in ("z x y", "x z y"):
        own, size = c * (n // 2) + y * (n // 8) + xl * (n // 16), n // 16
    else:
        own, size = (c * 2 + xl) * (n // 4), n // 4
    mine = piece.of(shard, (), own, size)
    land = piece.of(full, (z, xh), own, size)
    here = copies.here(mine, land)
    if plan == "plane":
        devices = [at.on_plane(i, k) for i, k in PLANE]
    elif plan == "facing y":
        devices = [at.on_z(k) for k in K3] + [at.facing(i) for i in range(4)]
    elif plan[0] == "z":
        devices = [at.on_z(k) for k in K3]
    else:
        devices = [at.on_x(k) for k in K3]
    first = [copies.remote(mine, land, device) for device in devices]
    started.extend(first)
    yield
    here.wait()
    for copy in first:
        copy.wait_recv()
    if plan == "plane":
        swap(piece.of(full, (EVERY, EVERY), c * (n // 2), n // 2))
        yield
    else:
        if plan in ("z x y", "x z y"):
            if plan == "z x y":
                view = piece.of(full, (EVERY, xh), own, size)
                second = [send(view, at.on_x(k)) for k in K3]
            else:
                view = piece.of(full, (z, EVERY), c * (n // 2) + y * (n // 8), n // 8)
                second = [send(view, at.on_z(k)) for k in K3]
            yield
            for copy in second:
                copy.wait_recv()
        if plan[-1] == "y":
            place, on = y, at.on_y

            def block(p, half=None):
                lead = EVERY if half is None else pl.ds(2 * half, 2)
                return piece.of(full, (lead, EVERY), c * (n // 2) + p * (n // 8), n // 8)

        elif plan[-1] == "x":
            place, on = at.x, at.on_x

            def block(p, half=None):
                lead = EVERY if half is None else pl.ds(2 * half, 2)
                return piece.of(full, (lead, p // 2), (c * 2 + p % 2) * (n // 4), n // 4)

        else:
            place, on = z, at.on_z

            def block(p, half=None):
                return piece.of(
                    full, (p, EVERY if half is None else half), c * (n // 2), n // 2
                )

        ahead, behind = (place + 1) % 4, (place + 3) % 4
        right = send(block(place), on(1))
        left = send(block(place), on(3))
        swap(block(place))
        yield
        right.wait_recv()
        more_right = send(block(behind, 0), on(1))
        left.wait_recv()
        more_left = send(block(ahead, 1), on(3))
        swap(block(behind))
        swap(block(ahead))
        yield
        more_right.wait_recv()
        more_left.wait_recv()
        swap(block((place + 2) % 4))
        yield
    for copy in swaps:
        copy.wait_recv()
    for copy in started:
        copy.wait_send()


SUM_PLAN = {
    "down": "z y x",
    "gate": "y x z",
    "up": "x y z",
    "out": "y x z whole",
    "q": "y x z whole",
    "kv": "plane",
    "gain": "plane",
}
SUM = tuple(SUM_PLAN)


def sum_scratch(name):
    plan, piece = SUM_PLAN[name], Piece(name)
    if plan == "plane":
        shapes = [((15,), 4), ((), 4), ((3,), 4)]
    elif plan == "z y x":
        shapes = [((3, 2), 2), ((2,), 2), ((3, 2), 8), ((2,), 8), ((3,), 16)]
    elif plan == "x y z":
        shapes = [((3, 4), 4), ((4,), 4), ((3, 4), 16), ((4,), 16), ((3,), 16)]
    elif plan == "y x z":
        shapes = [((3, 4, 2), 8), ((4, 2), 8), ((3, 4), 16), ((4,), 16), ((3,), 16)]
    else:
        shapes = [((3, 4, 2), 8), ((4, 2), 8), ((3, 4), 8), ((4,), 8), ((3,), 8)]
    return [piece.buffer(lead, part) for lead, part in [((4, 2), 2)] + shapes]


def sum_steps(at, copies, name, grad, result, landed, *buffers):
    piece = Piece(name)
    plan = SUM_PLAN[name]
    n = piece.extent
    z, xh, xl, y, c, x = at.z, at.xh, at.xl, at.y, at.c, at.x
    started = []

    def send(src, dst, device):
        started.append(copies.remote(src, dst, device))
        return started[-1]

    def add(own, arrived, target):
        value = own[...].astype(F32)
        for ref in arrived:
            value = value + ref[...].astype(F32)
        target[...] = value.astype(piece.kind)

    def over(dims, body):
        if not dims:
            body(())
        elif len(dims) == 1:
            lax.fori_loop(0, dims[0], lambda i, s: (body((i,)), s)[1], 0)
        else:
            lax.fori_loop(
                0, dims[0] * dims[1], lambda i, s: (body((i // dims[1], i % dims[1])), s)[1], 0
            )

    def arrive(going):
        for copy in going:
            copy.wait_recv()

    swap = send(
        piece.of(grad, (EVERY, EVERY), (1 - c) * (n // 2), n // 2), landed, at.other_core()
    )
    yield
    swap.wait_recv()
    over(
        (4, 2),
        lambda i: add(
            piece.of(grad, i, c * (n // 2), n // 2), [landed.at[i]], landed.at[i]
        ),
    )
    cut = piece.within
    if plan == "plane":
        land1, sum1, land2 = buffers
        going = []
        for j, (i, k) in enumerate(PLANE):
            xx = (x + k) % 4
            view = cut(landed, ((z + i) % 4, xx // 2), (xx % 2) * (n // 4), n // 4)
            going.append(send(view, land1.at[j], at.on_plane(i, k)))
        yield
        arrive(going)
        add(cut(landed, (z, xh), xl * (n // 4), n // 4), [land1.at[j] for j in range(15)], sum1)
        going = [send(sum1, land2.at[k - 1], at.on_y(k)) for k in K3]
        yield
        arrive(going)
        mine = piece.of(result, (), (c * 2 + xl) * (n // 4), n // 4)
        add(sum1, [land2.at[k - 1] for k in K3], mine)
        going = [send(mine, mine, device) for device in (at.pair(), at.other_core(), at.across())]
        yield
        arrive(going)
    else:
        land1, sum1, land2, sum2, land3 = buffers

        def phase(axis, pick, land, dims, target):
            place, on = {"x": (x, at.on_x), "y": (y, at.on_y), "z": (z, at.on_z)}[axis]
            going = [send(pick(EVERY, (place + k) % 4), land.at[k - 1], on(k)) for k in K3]
            yield
            arrive(going)
            over(
                dims,
                lambda i: add(pick(i, place), [land.at[(k - 1, *i)] for k in K3], target(i)),
            )

        def lead(i, rest):
            count = sum(r is None for r in rest)
            i = [EVERY] * count if i is EVERY else list(i)
            return tuple(i.pop(0) if r is None else r for r in rest)

        eighth, sixteenth = n // 8, n // 16
        if plan == "z y x":
            yield from phase(
                "z",
                lambda i, p: cut(landed, lead(i, (p, None)), 0, n // 2),
                land1,
                (2,),
                lambda i: sum1.at[i],
            )
            yield from phase(
                "y",
                lambda i, p: cut(sum1, lead(i, (None,)), p * eighth, eighth),
                land2,
                (2,),
                lambda i: sum2.at[i],
            )
            place = c * (n // 2) + y * eighth + xl * sixteenth
            mine = piece.of(result, (), place, sixteenth)
            yield from phase(
                "x",
                lambda i, p: cut(sum2, (p // 2,), (p % 2) * sixteenth, sixteenth),
                land3,
                (),
                lambda i: mine,
            )
        elif plan == "x y z":
            yield from phase(
                "x",
                lambda i, p: cut(landed, lead(i, (None, p // 2)), (p % 2) * (n // 4), n // 4),
                land1,
                (4,),
                lambda i: sum1.at[i],
            )
            yield from phase(
                "y",
                lambda i, p: cut(sum1, lead(i, (None,)), p * sixteenth, sixteenth),
                land2,
                (4,),
                lambda i: sum2.at[i],
            )
            place = c * (n // 2) + xl * (n // 4) + y * sixteenth
            mine = piece.of(result, (), place, sixteenth)
            yield from phase("z", lambda i, p: sum2.at[p], land3, (), lambda i: mine)
        else:
            yield from phase(
                "y",
                lambda i, p: cut(landed, lead(i, (None, None)), p * eighth, eighth),
                land1,
                (4, 2),
                lambda i: sum1.at[i],
            )
            if plan == "y x z":
                size = sixteenth
                place = c * (n // 2) + y * eighth + xl * sixteenth

                def pick(i, p):
                    return cut(sum1, lead(i, (None, p // 2)), (p % 2) * size, size)

            else:
                size = eighth
                place = c * (n // 2) + y * eighth

                def pick(i, p):
                    return sum1.at[lead(i, (None, p // 2))]

            yield from phase("x", pick, land2, (4,), lambda i: sum2.at[i])
            mine = piece.of(result, (), place, size)
            yield from phase("z", lambda i, p: sum2.at[p], land3, (), lambda i: mine)
        if plan == "x y z":
            going = [send(mine, mine, at.on_y(k)) for k in K3]
            yield
            arrive(going)
            wide = piece.of(result, (), c * (n // 2) + xl * (n // 4), n // 4)
            going = [send(wide, wide, at.pair())]
            yield
            arrive(going)
        else:
            if plan != "y x z whole":
                going = [send(mine, mine, at.pair())]
                yield
                arrive(going)
            wide = piece.of(result, (), c * (n // 2) + y * eighth, eighth)
            going = [send(wide, wide, at.on_y(k)) for k in K3]
            yield
            arrive(going)
        whole = piece.of(result, (), c * (n // 2), n // 2)
        going = [send(whole, whole, at.other_core())]
        yield
        arrive(going)
    for copy in started:
        copy.wait_send()


def run_all(steps):
    steps = list(steps)
    while steps:
        left = []
        for step in steps:
            try:
                next(step)
                left.append(step)
            except StopIteration:
                pass
        steps = left


def spread_gains(values):
    lead = values.shape[:-1]
    rows = values.reshape(*lead, 3, 1, 128)
    rows = jnp.pad(rows, [(0, 0)] * len(lead) + [(0, 1), (0, 7), (0, 0)])
    return rows.reshape(*lead, 32, 128)


def packed_gains(rows):
    lead = rows.shape[:-2]
    return rows.reshape(*lead, 4, 8, 128)[..., :3, 0, :].reshape(*lead, 384)


def rotary_tables(positions):
    freqs = 1000000.0 ** (-(jnp.arange(HD // 2, dtype=jnp.float32) * 2.0 / HD))
    angles = positions.astype(jnp.float32)[:, None] * freqs[None, :]
    return (jnp.cos(angles), jnp.sin(angles))


NN = (((1,), (0,)), ((), ()))
NT = (((1,), (1,)), ((), ()))
TN = (((0,), (0,)), ((), ()))
WIDE = 512


def mul(left, right, dims=NN):
    return lax.dot_general(left, right, dims, preferred_element_type=F32)


def inverse_rms(values):
    return lax.rsqrt(jnp.mean(values * values, axis=-1, keepdims=True) + norm_epsilon)


def norm_back(grad, hat, inverse, gain):
    scaled = grad * gain
    inner = jnp.mean(scaled * hat, axis=-1, keepdims=True)
    return jnp.sum(grad * hat, axis=0, keepdims=True), (scaled - hat * inner) * inverse


def turn(values, cosine, sine):
    half = values.shape[-1] // 2
    u, w = values[:, :half], values[:, half:]
    return jnp.concatenate([u * cosine - w * sine, w * cosine + u * sine], axis=1)


def gain_row(gain_ref, first, count):
    pieces = []
    for chunk in range(first, first + count):
        opt, row = chunk // 3, (chunk % 3) * 8
        pieces.append(gain_ref[opt // 2, opt % 2, row : row + 1, :])
    return jnp.concatenate(pieces, axis=1)


def put_gain(gain_ref, first, count, row_values):
    for i in range(count):
        chunk = first + i
        opt, row = chunk // 3, (chunk % 3) * 8
        gain_ref[opt // 2, opt % 2, row : row + 1, :] = row_values[:, i * 128 : (i + 1) * 128]


def step_kernel(*refs):
    x, ct, cosine, sine, pos = refs[:5]
    exact = dict(zip(ARRAYS, refs[5:10]))
    out, in_grad = refs[10:12]
    results = dict(zip(ARRAYS, refs[12:17]))
    rest = list(refs[17:])

    def take(n):
        taken = rest[:n]
        del rest[:n]
        return taken

    weights = dict(zip(ARRAYS, take(5)))
    grads = dict(zip(ARRAYS, take(5)))
    shards = dict(zip(ARRAYS, take(5)))
    landing = {name: take(len(sum_scratch(name))) for name in SUM}
    qkv, q_b, kv_all, o_acc, l_sum, o_b = take(6)
    branch, middle, gate, up, hidden, ffn, normed, down = take(8)
    do_b, dkv, landed, dqkv, reach = take(5)
    send, recv, kv_send, kv_recv, dkv_send, dkv_recv, load = take(7)
    dq, d_mid, d_ffn = o_acc, middle, in_grad
    at = Place()
    me = at.z * 2 + at.xh
    loads = [
        (exact["qkv"], gate.at[:80, :1536], shards["qkv"]),
        (exact["gu"].at[:, :FF], gate.at[80:160], shards["gu"].at[:, :FF]),
        (exact["gu"].at[:, FF:], gate.at[160:240], shards["gu"].at[:, FF:]),
        (exact["out"], up.at[:128, :D], shards["out"]),
        (exact["down"], up.at[:, D : 2 * D], shards["down"]),
    ]
    loads = [
        (pltpu.make_async_copy(source, stage, load.at[i]), stage, target)
        for i, (source, stage, target) in enumerate(loads)
    ]
    for copy, _, _ in loads:
        copy.start()
    shards["gain"][...] = exact["gain"][...]
    for copy, stage, target in loads:
        copy.wait()
        target[...] = stage[...].astype(LOW)
    greet(everyone(at))
    copies = Copies(send, recv)
    fetch = {
        t: gather_steps(at, copies, t, shards[PIECES[t][0]], weights[PIECES[t][0]])
        for t in GATHER_PLAN
    }

    def go(steps):
        next(steps, None)

    def member(opt):
        return at.device(z=opt // 2, xh=opt % 2)

    for t in ("kv", "gain", "q", "gate", "down", "out", "up"):
        go(fetch[t])
    tokens = x.shape[0]
    shift = lax.broadcasted_iota(jnp.int32, (tokens, tokens), 0) - lax.broadcasted_iota(
        jnp.int32, (tokens, tokens), 1
    )
    limit = jnp.transpose(jnp.broadcast_to(pos[...].astype(F32), (tokens, tokens)))
    reach[...] = shift - limit.astype(jnp.int32)
    xs = x[...]
    inv_x = inverse_rms(xs)
    x_hat = xs * inv_x
    for t in ("q", "gate", "down", "gain", "kv", "out", "up", "gain"):
        go(fetch[t])
    gain = weights["gain"]
    normed[...] = (x_hat * gain_row(gain, 0, 5)).astype(LOW)
    go(fetch["kv"])
    w_qkv, w_out, w_gu, w_down = (weights[t] for t in ("qkv", "out", "gu", "down"))

    low_in = normed[...]
    kv_cols = mul(low_in, w_qkv[:, :, :, 1024:1536].reshape(D, 512))
    qkv[:, 1024:1280] = kv_cols[:, :HD]
    keys = kv_cols[:, :HD]
    k_low = turn(keys * inverse_rms(keys) * gain_row(gain, 22, 2), cosine[...], sine[...]).astype(LOW)
    kv_all[me] = jnp.concatenate([k_low, kv_cols[:, HD:].astype(LOW)], axis=1)

    def kv_copy(k, slot, opt):
        return pltpu.make_async_remote_copy(
            src_ref=kv_all.at[slot],
            dst_ref=kv_all.at[slot],
            send_sem=kv_send.at[k],
            recv_sem=kv_recv.at[k],
            device_id=member(opt),
            device_id_type=MESH,
        )

    for k in range(1, 8):

        @pl.when(me + k < 8)
        def _():
            kv_copy(k, me, me + k).start()

    for t in ("gate", "down", "q", "q", "q"):
        go(fetch[t])
    g_query = gain_row(gain, 20, 2)
    for part in range(2):
        cols = mul(low_in, w_qkv[:, :, :, part * 512 : part * 512 + 512].reshape(D, 512))
        qkv[:, part * 512 : part * 512 + 512] = cols
        for i in range(2):
            q = cols[:, i * HD : (i + 1) * HD]
            q = turn(q * inverse_rms(q) * g_query, cosine[...], sine[...]).astype(LOW)
            q_b[part * 2 + i] = q * jnp.asarray(HD**-0.5, LOW)

    o_acc[...] = jnp.zeros_like(o_acc)
    l_sum[...] = jnp.zeros_like(l_sum)
    def allowed(k):
        return (shift >= -k * tokens) & (reach[...] <= -k * tokens)

    def forward_block(k, carry):
        @pl.when(k > 0)
        def _():
            kv_copy(k, me - k, me - k).wait_recv()

        kv = kv_all[me - k]
        ok = allowed(k)
        for h in range(HQ):
            s = mul(q_b[h], kv[:, :HD], NT)
            e = jnp.where(ok, jnp.exp(s), 0.0)
            l_sum[h] += e[:, :128] + e[:, 128:]
            o_acc[h] += mul(e.astype(LOW), kv[:, HD:])
        return carry

    def blocks(body, low_k, high_k):
        lax.fori_loop(low_k, jnp.minimum(me + 1, high_k), body, 0)

    blocks(forward_block, 0, 1)
    go(fetch["out"])
    go(fetch["gate"])
    blocks(forward_block, 1, 8)
    for t in ("out", "up", "gate", "down", "up"):
        go(fetch[t])
    for h in range(HQ):
        l_inv = 1.0 / jnp.sum(l_sum[h], axis=-1, keepdims=True)
        o = o_acc[h] * l_inv
        o_acc[h] = o
        l_sum[h] = jnp.broadcast_to(l_inv, (tokens, 128))
        o_b[:, h * HD : (h + 1) * HD] = o.astype(LOW)
    go(fetch["out"])
    r = mul(o_b[...], w_out[...].reshape(HQ * HD, D))
    branch[...] = r
    x1 = x[...] + r * inverse_rms(r) * gain_row(gain, 5, 5)
    middle[...] = x1
    ffn[...] = (x1 * inverse_rms(x1) * gain_row(gain, 10, 5)).astype(LOW)
    for t in ("down", "gate", "up", "down"):
        go(fetch[t])

    root = 0.7978845608028654

    def up_chunk(i, carry):
        cols = pl.ds(pl.multiple_of(i * WIDE, WIDE), WIDE)
        more = pl.ds(pl.multiple_of(FF + i * WIDE, WIDE), WIDE)
        b = ffn[...]
        z = mul(b, w_gu[:, :, :, cols].reshape(D, WIDE))
        u = mul(b, w_gu[:, :, :, more].reshape(D, WIDE))
        t = jnp.tanh(root * (z + 0.044715 * z * z * z))
        gelu = 0.5 * z * (1.0 + t)
        slope = 0.5 * (1.0 + t) + 0.5 * z * (1.0 - t * t) * root * (1.0 + 3.0 * 0.044715 * z * z)
        gate[:, cols] = slope * u
        up[:, cols] = gelu
        hidden[:, cols] = (gelu * u).astype(LOW)
        return carry

    lax.fori_loop(0, FF // WIDE, up_chunk, 0)
    m = mul(hidden[...], w_down[...].reshape(FF, D))
    inv_m = inverse_rms(m)
    m_hat = m * inv_m
    g_out = gain_row(gain, 15, 5)
    out[...] = middle[...] + m_hat * g_out
    total = {
        t: sum_steps(at, copies, t, grads[PIECES[t][0]], results[PIECES[t][0]], *landing[t])
        for t in SUM
    }
    grad_gain = grads["gain"]
    grad_gain[...] = jnp.zeros_like(grad_gain)
    grad_row, dm = norm_back(ct[...], m_hat, inv_m, g_out)
    put_gain(grad_gain, 15, 5, grad_row)
    down[...] = dm.astype(LOW)

    def down_grad(i, carry):
        cols = pl.ds(pl.multiple_of(i * WIDE, WIDE), WIDE)
        grads["down"][i] = mul(hidden[:, cols], down[...], TN).astype(LOW).reshape(2, 256, D)
        return carry

    lax.fori_loop(0, FF // WIDE, down_grad, 0)
    go(total["down"])

    d_ffn[...] = jnp.zeros_like(d_ffn)

    def down_chunk(i, carry):
        cols = pl.ds(pl.multiple_of(i * WIDE, WIDE), WIDE)
        more = pl.ds(pl.multiple_of(FF + i * WIDE, WIDE), WIDE)
        dm_b, b = down[...], ffn[...]
        dh = mul(dm_b, w_down[i].reshape(WIDE, D), NT)
        d_gate = (dh * gate[:, cols]).astype(LOW)
        d_up = (dh * up[:, cols]).astype(LOW)
        grads["gu"][:, :, :, cols] = mul(b, d_gate, TN).astype(LOW).reshape(4, 2, 80, WIDE)
        grads["gu"][:, :, :, more] = mul(b, d_up, TN).astype(LOW).reshape(4, 2, 80, WIDE)
        d_ffn[...] += mul(d_gate, w_gu[:, :, :, cols].reshape(D, WIDE), NT) + mul(
            d_up, w_gu[:, :, :, more].reshape(D, WIDE), NT
        )
        return carry

    lax.fori_loop(0, FF // WIDE, down_chunk, 0)
    go(total["gate"])
    go(total["up"])
    go(total["down"])
    x1 = middle[...]
    inv_1 = inverse_rms(x1)
    grad_row, dx = norm_back(d_ffn[...], x1 * inv_1, inv_1, gain_row(gain, 10, 5))
    put_gain(grad_gain, 10, 5, grad_row)
    dx = ct[...] + dx
    d_mid[...] = dx
    r = branch[...]
    inv_r = inverse_rms(r)
    grad_row, dr = norm_back(dx, r * inv_r, inv_r, gain_row(gain, 5, 5))
    put_gain(grad_gain, 5, 5, grad_row)
    dr_b = dr.astype(LOW)
    for h in range(HQ):
        grads["out"][h] = mul(o_b[:, h * HD : (h + 1) * HD], dr_b, TN).astype(LOW).reshape(2, 128, D)
        do_b[h] = mul(dr_b, w_out[h].reshape(HD, D), NT).astype(LOW)
    go(total["out"])
    go(total["gate"])
    go(total["up"])
    for h in range(HQ):
        delta = jnp.sum(o_acc[h] * do_b[h].astype(F32), axis=-1, keepdims=True)
        l_sum[h, :, 64:] = jnp.broadcast_to(delta, (tokens, 64))
    go(total["out"])
    dq[...] = jnp.zeros_like(dq)

    def back_block(k):
        kv = kv_all[me - k]
        keys, values = kv[:, :HD], kv[:, HD:]
        ok = allowed(k)
        d_keys = d_values = None
        for h in range(HQ):
            s = mul(q_b[h], keys, NT)
            p = jnp.where(ok, jnp.exp(s) * l_sum[h, :, :1], 0.0)
            dp = mul(do_b[h], values, NT)
            ds = (p * (dp - l_sum[h, :, 64:65])).astype(LOW)
            dq[h] += mul(ds, keys)
            more_keys = mul(ds, q_b[h], TN)
            more_values = mul(p.astype(LOW), do_b[h], TN)
            d_keys = more_keys if h == 0 else d_keys + more_keys
            d_values = more_values if h == 0 else d_values + more_values
        return d_keys, d_values

    def dkv_copy(k, opt):
        return pltpu.make_async_remote_copy(
            src_ref=kv_all.at[opt],
            dst_ref=landed.at[k - 1],
            send_sem=dkv_send.at[k],
            recv_sem=dkv_recv.at[k],
            device_id=member(opt),
            device_id_type=MESH,
        )

    def away_block(k, carry):
        d_keys, d_values = back_block(k)
        kv_all[me - k, :, :HD] = d_keys.astype(LOW)
        kv_all[me - k, :, HD:] = d_values.astype(LOW)
        dkv_copy(k, me - k).start()
        return carry

    blocks(away_block, 1, 8)
    d_keys, d_values = back_block(0)
    dkv[:, :HD] = d_keys
    dkv[:, HD:] = d_values

    grad_row = None
    for h in range(HQ):
        q = qkv[:, h * HD : (h + 1) * HD]
        inv_q = inverse_rms(q)
        e = turn(dq[h] * HD**-0.5, cosine[...], -sine[...])
        more, back = norm_back(e, q * inv_q, inv_q, g_query)
        grad_row = more if h == 0 else grad_row + more
        dqkv[:, h * HD : (h + 1) * HD] = back.astype(LOW)
    put_gain(grad_gain, 20, 2, grad_row)
    low_in = normed[...]
    for part in range(2):
        cols = slice(part * 512, part * 512 + 512)
        grads["qkv"][:, :, :, cols] = mul(low_in, dqkv[:, cols], TN).astype(LOW).reshape(4, 2, 80, 512)
    go(total["q"])
    for t in ("down", "gate", "out", "q", "up"):
        go(total[t])

    def arrived(k, carry):
        dkv_copy(k, me + k).wait_recv()
        dkv[...] += landed[k - 1].astype(F32)
        return carry

    lax.fori_loop(1, 8 - me, arrived, 0)
    keys = qkv[:, 1024:1280]
    inv_k = inverse_rms(keys)
    e = turn(dkv[:, :HD], cosine[...], -sine[...])
    grad_row, back = norm_back(e, keys * inv_k, inv_k, gain_row(gain, 22, 2))
    put_gain(grad_gain, 22, 2, grad_row)
    dqkv[:, 1024:1280] = back.astype(LOW)
    dqkv[:, 1280:1536] = dkv[:, HD:].astype(LOW)
    grads["qkv"][:, :, :, 1024:1536] = (
        mul(low_in, dqkv[:, 1024:1536], TN).astype(LOW).reshape(4, 2, 80, 512)
    )
    go(total["kv"])
    d_normed = mul(dqkv[...], w_qkv[...].reshape(D, 1536), NT)
    xs = x[...]
    inv_x = inverse_rms(xs)
    grad_row, back = norm_back(d_normed, xs * inv_x, inv_x, gain_row(gain, 0, 5))
    put_gain(grad_gain, 0, 5, grad_row)
    go(total["gain"])
    go(total["kv"])
    in_grad[...] = d_mid[...] + back
    go(total["gain"])
    for k in range(1, 8):

        @pl.when(me + k < 8)
        def _():
            kv_copy(k, me, me + k).wait_send()

        @pl.when(me - k >= 0)
        def _():
            dkv_copy(k, me - k).wait_send()

    run_all([*fetch.values()])
    run_all([total[t] for t in ("down", "kv", "gain", "gate", "out", "q", "up")])


def one_step(inputs, cotangent, cosine, sine, positions, shards):
    vmem = pl.BlockSpec(memory_space=pltpu.VMEM)
    hbm = pl.BlockSpec(memory_space=pltpu.HBM)
    tokens = inputs.shape[0]

    def shard(t, lead=()):
        rows, cols, kind = ARRAYS[t]
        return pltpu.VMEM((*lead, rows, cols), kind)

    scratch = [shard(t, (4, 2)) for t in ARRAYS] * 2 + [shard(t) for t in ARRAYS]
    for t in SUM:
        scratch += sum_scratch(t)
    scratch += [
        pltpu.VMEM((tokens, 1280), F32),
        pltpu.VMEM((HQ, tokens, HD), LOW),
        pltpu.VMEM((8, tokens, 2 * HD), LOW),
        pltpu.VMEM((HQ, tokens, HD), F32),
        pltpu.VMEM((HQ, tokens, 128), F32),
        pltpu.VMEM((tokens, HQ * HD), LOW),
        pltpu.VMEM((tokens, D), F32),
        pltpu.VMEM((tokens, D), F32),
        pltpu.VMEM((tokens, FF), F32),
        pltpu.VMEM((tokens, FF), F32),
        pltpu.VMEM((tokens, FF), LOW),
        pltpu.VMEM((tokens, D), LOW),
        pltpu.VMEM((tokens, D), LOW),
        pltpu.VMEM((tokens, D), LOW),
        pltpu.VMEM((HQ, tokens, HD), LOW),
        pltpu.VMEM((tokens, 2 * HD), F32),
        pltpu.VMEM((7, tokens, 2 * HD), LOW),
        pltpu.VMEM((tokens, 1536), LOW),
        pltpu.VMEM((tokens, tokens), jnp.int32),
        pltpu.SemaphoreType.DMA((256,)),
        pltpu.SemaphoreType.DMA((256,)),
    ] + [pltpu.SemaphoreType.DMA((8,))] * 5
    outs = pl.pallas_call(
        step_kernel,
        name="one_step",
        out_shape=[jax.ShapeDtypeStruct((tokens, D), F32)] * 2
        + [jax.ShapeDtypeStruct((rows, cols), kind) for rows, cols, kind in ARRAYS.values()],
        in_specs=[vmem] * 5 + [hbm, vmem, hbm, hbm, hbm],
        out_specs=[vmem] * 7,
        scratch_shapes=scratch,
        compiler_params=pltpu.CompilerParams(
            collective_id=1, has_side_effects=True, vmem_limit_bytes=62 * 2**20
        ),
    )(inputs, cotangent, cosine, sine, positions, *[shards[t] for t in ARRAYS])
    return outs[0], outs[1], dict(zip(ARRAYS, outs[2:]))


def adamw(weight, gradient, first, second, step_rate, weight_decay):
    new_first = 0.9 * first + 0.1 * gradient
    new_second = 0.999 * second + 0.001 * gradient * gradient
    first_hat = new_first / (1.0 - 0.9**STEP)
    second_hat = new_second / (1.0 - 0.999**STEP)
    new_weight = weight - step_rate * (
        first_hat / (jnp.sqrt(second_hat) + 1e-08) + weight_decay * weight
    )
    return (new_weight, new_first, new_second)


def local(
    inputs,
    cotangent,
    positions,
    w_qkv,
    w_out,
    w_gate_up,
    w_down,
    gains,
    first_qkv,
    first_out,
    first_gate_up,
    first_down,
    first_gains,
    second_qkv,
    second_out,
    second_gate_up,
    second_down,
    second_gains,
):
    cosine, sine = rotary_tables(positions)
    output, input_grad, result = one_step(
        inputs,
        cotangent,
        cosine,
        sine,
        positions[None, :],
        {
            "qkv": w_qkv,
            "out": w_out,
            "gu": w_gate_up,
            "down": w_down,
            "gain": spread_gains(gains.astype(LOW).astype(F32)),
        },
    )
    summed = tuple(result[t].astype(F32) for t in ("qkv", "out", "gu", "down")) + (
        packed_gains(result["gain"]),
    )
    params = (w_qkv, w_out, w_gate_up, w_down, gains)
    firsts = (first_qkv, first_out, first_gate_up, first_down, first_gains)
    seconds = (second_qkv, second_out, second_gate_up, second_down, second_gains)
    rates = (D ** (-0.5), (HQ * HD) ** (-0.5), D ** (-0.5), FF ** (-0.5), 0.8)
    decays = (0.01, 0.01, 0.01, 0.01, 0.0)
    updated = [
        adamw(params[idx], summed[idx], firsts[idx], seconds[idx], rates[idx], decays[idx])
        for idx in range(5)
    ]
    return (
        output,
        input_grad,
        updated[0][0],
        updated[1][0],
        updated[2][0],
        updated[3][0],
        updated[4][0],
        updated[0][1],
        updated[1][1],
        updated[2][1],
        updated[3][1],
        updated[4][1],
        updated[0][2],
        updated[1][2],
        updated[2][2],
        updated[3][2],
        updated[4][2],
    )


def solution(mesh):
    placed = (
        P(("dp", "opt"), None),
        P(("dp", "opt"), None),
        P(("dp", "opt")),
        P("opt", None),
        P("opt", None),
        P("opt", None),
        P("opt", None),
        P("opt"),
        P("opt", None),
        P("opt", None),
        P("opt", None),
        P("opt", None),
        P("opt"),
        P("opt", None),
        P("opt", None),
        P("opt", None),
        P("opt", None),
        P("opt"),
    )
    return jax.shard_map(
        local,
        mesh=mesh,
        in_specs=placed,
        out_specs=(
            P(("dp", "opt"), None),
            P(("dp", "opt"), None),
            P("opt", None),
            P("opt", None),
            P("opt", None),
            P("opt", None),
            P("opt"),
            P("opt", None),
            P("opt", None),
            P("opt", None),
            P("opt", None),
            P("opt"),
            P("opt", None),
            P("opt", None),
            P("opt", None),
            P("opt", None),
            P("opt"),
        ),
        check_vma=False,
    )
```
